32 devices in a mesh: dp: 4 (over z), expert: 8 (over y, x, core).
Axes of the slice: x: 2, y: 2, z: 4, core: 2. Of those that a mesh axis runs over, the one named last changes fastest.
Arguments:
- tokens: bfloat16 [8192, 1280], P(('dp', 'expert')), may hold values from -6 to 6
- expert_ids: int32 [8192, 2], P(('dp', 'expert')), may hold values from 0 to 15, all different within a row; in each aligned block of 256 rows (0 to 255, 256 to 511, ...) at most 48 rows name the same one
- gate_weights: float32 [8192, 2], P(('dp', 'expert')), may hold values from 0.1 to 1
- target: int32 [8192], P(('dp', 'expert')), may hold values from 0 to 8191, as said below
- expert_gate: bfloat16 [16, 1280, 1024], P('expert'), may hold values from -0.15625 to 0.15625
- expert_up: bfloat16 [16, 1280, 1024], P('expert'), may hold values from -0.15625 to 0.15625
- expert_down: bfloat16 [16, 1024, 1280], P('expert'), may hold values from -0.1875 to 0.1875
- dec_embed: bfloat16 [1280, 512], replicated, may hold values from -0.15625 to 0.15625
- mask_token: bfloat16 [512], replicated, may hold values from -5 to 5
- norm_gain: float32 [512], replicated, may hold values from 0.1 to 1.9
- w_qkv: bfloat16 [512, 1536], replicated, may hold values from -0.25 to 0.25
- w_out: bfloat16 [512, 512], replicated, may hold values from -0.25 to 0.25
- w_head: bfloat16 [512, 768], replicated, may hold values from -0.25 to 0.25
- pixels: bfloat16 [32, 1024, 768], P('dp', 'expert'), may hold values from -60 to 60
Outputs:
- decoded: bfloat16 [32, 1024, 512], P('dp', 'expert')
- d_attn: bfloat16 [32, 1024, 512], P('dp', 'expert')
- tile_loss: float32 [4, 8], P('dp', 'expert')
The draws below stay inside these ranges and needn't reach their ends.
Inputs may be any that keep to these rules, and one draw needn't show every extreme that they name: `expert_ids`: each row names 2 different experts. Among the 256 rows of one device no expert is named more than 48 times, a bound that some block reaches; every expert is named somewhere. target = j * 1024 + q names tile j of the token's dp group and patch q of that tile. No two tokens of one dp group share a value. The 256 tokens of one device name any one tile at most 128 times, and some tile exactly 128 times.
All inputs are finite; a program needn't handle non-finite values.
Results may differ from the reference program's by a relative error of at most 0.012.
Values may be sent and summed in bfloat16 or wider, within the bound.
No kernel may reach another device: no remote copies, remote signals or barrier semaphores. Data moves between devices by JAX's collectives and lax.ppermute only.
A program may use at most 384 MiB of HBM per device.

```python
import math
import jax
import jax.numpy as jnp
import numpy as np
from jax import lax

D = 1280
FE = 1024
TOPK = 2
DD = 512
HD = 32
PD = 768
RAD = 3
TW = 128
TOK_DEV = 256
EXPERTS = 16
TOKENS = 8192
TILE = 1024
TH = 8
GH = 32
GW = 1024
CAPE = 48
CAPR = 128
N_DP = 4
N_EXPERT = 8
DEVICES = 32


def source_tiles(source_key):
    key_order, key_noise, key_shuffle = jax.random.split(source_key, 3)
    slots_all = N_EXPERT * CAPR
    tile_order = jax.random.permutation(key_order, N_EXPERT).astype(jnp.int32)
    noise_draw = jax.random.randint(key_noise, (slots_all,), 0, 1 << 18, dtype=jnp.int32)
    places = jnp.arange(slots_all, dtype=jnp.int32)
    scores = jnp.where(places < CAPR, places - slots_all, noise_draw * slots_all + places)
    chosen = jnp.argsort(scores)[:TOK_DEV]
    tile_list = tile_order[chosen // CAPR]
    return tile_list[jax.random.permutation(key_shuffle, TOK_DEV)]


def tile_patches(patch_key):
    return jax.random.permutation(patch_key, TILE).astype(jnp.int32)


def draw_target(key, part):
    source_keys = jax.random.split(jax.random.fold_in(key, 7), DEVICES)
    tile_list = jax.vmap(source_tiles)(source_keys).reshape(N_DP, N_EXPERT * TOK_DEV)
    one_hot = (tile_list[:, :, None] == jnp.arange(N_EXPERT, dtype=jnp.int32)[None, None, :]).astype(jnp.int32)
    rank_in = jnp.sum((jnp.cumsum(one_hot, axis=1) - 1) * one_hot, axis=2)
    patch_keys = jax.random.split(jax.random.fold_in(key, 9), N_DP * N_EXPERT)
    patch_orders = jax.vmap(tile_patches)(patch_keys).reshape(N_DP, N_EXPERT, TILE)
    group_ids = jnp.arange(N_DP, dtype=jnp.int32)[:, None]
    patches = patch_orders[group_ids, tile_list, rank_in]
    return (tile_list * TILE + patches).reshape(TOKENS).astype(jnp.int32)


def draw_pixels(key, part):
    key_base, key_rows, key_cols, key_shift = jax.random.split(jax.random.fold_in(key, 5), 4)
    base_part = jnp.clip(jax.random.normal(key_base, (GH, GW, PD), jnp.float32), -4.0, 4.0)
    row_scale = jnp.exp(jax.random.uniform(key_rows, (GH, GW, 1), jnp.float32, math.log(0.3), math.log(3.0)))
    col_scale = jnp.exp(jax.random.uniform(key_cols, (PD,), jnp.float32, math.log(0.3), math.log(3.0)))
    shift_part = jnp.clip(jax.random.normal(key_shift, (GH, GW, 1), jnp.float32), -3.0, 3.0)
    return (base_part * row_scale * col_scale[None, None, :] + shift_part).astype(jnp.bfloat16)


def block_levels(key, extent, shards, least, top_value):
    loudness = 1.0
    for dim, parts in shards:
        draws = jax.random.uniform(jax.random.fold_in(jax.random.fold_in(key, 6), dim), (parts,), jnp.float32, least / len(shards), top_value / len(shards))
        loudness = loudness * jnp.repeat(jnp.exp(draws), extent[dim] // parts).reshape((-1,) + (1,) * (len(extent) - 1 - dim))
    return loudness


def routed_block(own_key, own, number, rows, count, top, reach, skew):
    ranking = jax.random.permutation(own_key, count)
    packed, usual = portions_of(count, rows * top, reach, skew, True), portions_of(count, rows * top, reach, skew, False)
    places = jnp.arange(count)

    def named(sizes, turn):
        used = int((sizes > 0).sum())
        fixed = max(1, used // 4)
        shifted = fixed + (places - fixed + turn * (used - fixed)) % max(1, count - fixed)
        return jnp.zeros((count,), jnp.int32).at[ranking[jnp.where(places < fixed, places, shifted)]].set(jnp.asarray(sizes, jnp.int32))

    sizes = jnp.where(number % 4 == 0, named(packed, number // 4), named(usual, number - number // 4 - 1))
    mixed = jax.random.permutation(jax.random.fold_in(own, 3), count)
    donor, sink = mixed[0:count // 2 * 2:2], mixed[1:count // 2 * 2:2]
    margin = jnp.minimum(sizes[donor] - 1, reach - sizes[sink]) // 2
    margin = jnp.where((donor == ranking[0]) | (sink == ranking[0]) | (sizes[sink] == 0), 0, jnp.maximum(margin, 0))
    shifted = jax.random.randint(jax.random.fold_in(own, 4), (count // 2,), 0, 1 << 20) % (margin + 1)
    sizes = sizes.at[donor].add(-shifted).at[sink].add(shifted)
    items = jnp.searchsorted(jnp.cumsum(sizes), jnp.arange(rows * top), side="right").astype(jnp.int32)
    table = items.reshape(top, rows).T
    table = table[jax.random.permutation(jax.random.fold_in(own, 1), rows)]
    turn = jax.random.randint(jax.random.fold_in(own, 2), (rows, 1), 0, top)
    return jnp.take_along_axis(table, (jnp.arange(top)[None, :] + turn) % top, axis=1)


def portions_of(count, total, bound, skew, full):
    loads = [(1 << 20) // math.isqrt(grade ** skew) + 1 for grade in range(1, count + 1)]
    largest = bound if full else min(bound, max(-(-total // count), total * loads[0] // sum(loads)))
    least = 1 if total - largest >= count - 1 else 0
    given, rest = [largest] + [least] * (count - 1), total - largest - least * (count - 1)
    while rest > 0:
        candidates = [i for i in range(1, count) if given[i] < largest] or [i for i in range(1, count) if given[i] < bound]
        pool, remaining = sum([loads[i] for i in candidates]), rest
        for i in candidates:
            addition = min(bound - given[i], max(1, remaining * loads[i] // pool), rest)
            given[i] = given[i] + addition
            rest = rest - addition
    return np.array(given)


def scatter_about(rng, extent, width, reach, cuts=(), kind=jnp.bfloat16):
    values = jax.random.normal(rng, extent, jnp.float32) * width
    if len(cuts) > 0:
        values = block_levels(rng, extent, cuts, -0.22, 0.18) * values
    return jnp.clip(values, min=-reach, max=reach).astype(kind)


def setup_inputs(seed: int = 0) -> dict:
    streams_of = jax.random.split(jax.random.key(seed), 15)
    tokens = scatter_about(streams_of[0], (TOKENS, D), 1.0, 6.0, ((0, 32),))
    expert_ids_keys = jax.random.split(jax.random.fold_in(streams_of[1], 1), TOKENS // TOK_DEV)
    expert_ids_turns = jax.random.permutation(jax.random.fold_in(streams_of[1], 3), TOKENS // TOK_DEV)
    expert_ids = jax.vmap(lambda own, number: routed_block(jax.random.fold_in(streams_of[1], 2), own, number, TOK_DEV, EXPERTS, TOPK, CAPE, 2))(expert_ids_keys, expert_ids_turns).reshape((TOKENS, TOPK))
    gate_weights = jnp.clip(0.1 + 0.9 * jax.random.uniform(streams_of[2], (TOKENS, TOPK), jnp.float32) ** block_levels(streams_of[2], (TOKENS, TOPK), ((0, 32),), -0.2, 0.2), 0.1, 1.0)
    target = draw_target(jax.random.fold_in(streams_of[14], 71), 0)
    expert_gate = scatter_about(streams_of[4], (EXPERTS, D, FE), D ** -0.5, 0.15625, ((0, 8),))
    expert_up = scatter_about(streams_of[5], (EXPERTS, D, FE), D ** -0.5, 0.15625, ((0, 8),))
    expert_down = scatter_about(streams_of[6], (EXPERTS, FE, D), FE ** -0.5, 0.1875, ((0, 8),))
    dec_embed = scatter_about(streams_of[7], (D, DD), D ** -0.5, 0.15625)
    mask_token = scatter_about(streams_of[8], (DD,), 1.0, 5.0)
    norm_gain = jnp.clip(1.0 + 0.18 * jax.random.normal(streams_of[9], (DD,), jnp.float32), 0.1, 1.9)
    w_qkv = scatter_about(streams_of[10], (DD, 3 * DD), DD ** -0.5, 0.25)
    w_out = scatter_about(streams_of[11], (DD, DD), DD ** -0.5, 0.25)
    w_head = scatter_about(streams_of[12], (DD, PD), DD ** -0.5, 0.25)
    pixels = draw_pixels(jax.random.fold_in(streams_of[14], 71), 0)
    return {"tokens": tokens, "expert_ids": expert_ids, "gate_weights": gate_weights, "target": target, "expert_gate": expert_gate, "expert_up": expert_up, "expert_down": expert_down, "dec_embed": dec_embed, "mask_token": mask_token, "norm_gain": norm_gain, "w_qkv": w_qkv, "w_out": w_out, "w_head": w_head, "pixels": pixels}


EPSILON = 1e-06

def positional(row_ids, col_ids, total_width):
    quarter = total_width // 4
    frequency = jnp.exp(jnp.arange(quarter, dtype=jnp.float32) * (-math.log(10000.0) / quarter))
    row_angle = row_ids.astype(jnp.float32)[:, None] * frequency[None, :]
    col_angle = col_ids.astype(jnp.float32)[:, None] * frequency[None, :]
    height = row_angle.shape[0]
    breadth = col_angle.shape[0]
    row_part = jnp.broadcast_to(jnp.concatenate([jnp.sin(row_angle), jnp.cos(row_angle)], 1)[:, None, :], (height, breadth, 2 * quarter))
    col_part = jnp.broadcast_to(jnp.concatenate([jnp.sin(col_angle), jnp.cos(col_angle)], 1)[None, :, :], (height, breadth, 2 * quarter))
    return jnp.concatenate([row_part, col_part], 2)

def attend(queries, kv_padded, valid_padded):
    height, breadth, model_width = queries.shape
    heads = model_width // HD
    span = 2 * RAD + 1
    query_heads = queries.astype(jnp.float32).reshape(height, breadth, heads, HD)
    scale = 1.0 / math.sqrt(HD)
    weight_list = []
    for offset in range(span * span):
        row_shift = offset // span
        col_shift = offset % span
        key_rows = kv_padded[row_shift:row_shift + height, col_shift:col_shift + breadth, :model_width]
        key_heads = key_rows.astype(jnp.float32).reshape(height, breadth, heads, HD)
        raw_score = jnp.einsum('hwnc,hwnc->nhw', query_heads, key_heads) * scale
        valid_here = valid_padded[row_shift:row_shift + height, col_shift:col_shift + breadth]
        weight_list.append(jnp.exp(raw_score) * valid_here[None])
    stacked = jnp.stack(weight_list)
    attn_weights = (stacked / lax.optimization_barrier(jnp.sum(stacked, axis=0))).astype(jnp.bfloat16)
    total = jnp.zeros((height, breadth, heads, HD), jnp.float32)
    for offset in range(span * span):
        row_shift = offset // span
        col_shift = offset % span
        value_rows = kv_padded[row_shift:row_shift + height, col_shift:col_shift + breadth, model_width:]
        value_heads = value_rows.astype(jnp.float32).reshape(height, breadth, heads, HD)
        total = total + jnp.einsum('nhw,hwnc->hwnc', attn_weights[offset].astype(jnp.float32), value_heads)
    return total.reshape(height, breadth, model_width).astype(jnp.bfloat16)

def reference(tokens, expert_ids, gate_weights, target, expert_gate, expert_up, expert_down, dec_embed, mask_token, norm_gain, w_qkv, w_out, w_head, pixels):
    flat_ids = expert_ids.reshape(-1).astype(jnp.int32)
    assigned = TOKENS * TOPK
    capacity_all = DEVICES * CAPE

    def per_expert(expert_index):
        picks = jnp.nonzero(flat_ids == expert_index, size=capacity_all, fill_value=assigned)[0].astype(jnp.int32)
        source_rows = tokens[jnp.minimum(picks // TOPK, TOKENS - 1)]
        gate_part = jnp.dot(source_rows, expert_gate[expert_index], preferred_element_type=jnp.float32)
        up_part = jnp.dot(source_rows, expert_up[expert_index], preferred_element_type=jnp.float32)
        expert_hidden = (jax.nn.silu(gate_part) * up_part).astype(jnp.bfloat16)
        outcome = jnp.dot(expert_hidden, expert_down[expert_index], preferred_element_type=jnp.float32).astype(jnp.bfloat16)
        return (picks, outcome)
    picks, outcome = lax.map(per_expert, jnp.arange(EXPERTS, dtype=jnp.int32))
    expert_rows = jnp.zeros((assigned + 1, D), jnp.bfloat16).at[picks.reshape(-1)].set(outcome.reshape(-1, D))
    expert_rows = expert_rows[:assigned].reshape(TOKENS, TOPK, D)
    mixed = tokens.astype(jnp.float32)
    for slot_index in range(TOPK):
        mixed = mixed + gate_weights[:, slot_index, None] * expert_rows[:, slot_index].astype(jnp.float32)
    moe_out = mixed.astype(jnp.bfloat16)
    embedded = jnp.dot(moe_out, dec_embed, preferred_element_type=jnp.float32).astype(jnp.bfloat16)
    token_index = jnp.arange(TOKENS, dtype=jnp.int32)
    group_index = token_index // (TOK_DEV * N_EXPERT)
    tile_index = target // TILE
    within_tile = target % TILE
    grid_rows = group_index * TH + within_tile // TW
    grid_cols = tile_index * TW + within_tile % TW
    flat_place = (grid_rows * GW + grid_cols).astype(jnp.int32)
    visible = jnp.zeros((GH * GW, DD), jnp.bfloat16).at[flat_place].set(embedded)
    keep = jnp.zeros((GH * GW,), jnp.float32).at[flat_place].set(1.0)
    position = positional(jnp.arange(GH, dtype=jnp.int32), jnp.arange(GW, dtype=jnp.int32), DD).reshape(GH * GW, DD)
    decoder_in = jnp.where(keep[:, None] > 0.5, visible.astype(jnp.float32), mask_token.astype(jnp.float32)[None, :]) + position
    mean_square = lax.optimization_barrier(jnp.mean(decoder_in * decoder_in, axis=1, keepdims=True))
    normed = (decoder_in * lax.rsqrt(mean_square + EPSILON) * norm_gain[None, :]).astype(jnp.bfloat16)
    projected = jnp.dot(normed, w_qkv, preferred_element_type=jnp.float32).astype(jnp.bfloat16).reshape(GH, GW, 3 * DD)
    query_grid = projected[:, :, :DD]
    kv_all = jnp.pad(projected[:, :, DD:], ((RAD, RAD), (RAD, RAD), (0, 0)))
    valid_all = jnp.pad(jnp.ones((GH, GW), jnp.float32), RAD)
    decoder_grid = decoder_in.reshape(GH, GW, DD)
    keep_grid = keep.reshape(GH, GW)

    def band_work(band_index):
        band_start = (band_index * TH).astype(jnp.int32)
        queries = lax.dynamic_slice_in_dim(query_grid, band_start, TH, 0)
        kv_band = lax.dynamic_slice_in_dim(kv_all, band_start, TH + 2 * RAD, 0)
        valid_band = lax.dynamic_slice_in_dim(valid_all, band_start, TH + 2 * RAD, 0)
        attended = attend(queries, kv_band, valid_band).reshape(TH * GW, DD)
        inputs_band = lax.dynamic_slice_in_dim(decoder_grid, band_start, TH, 0).reshape(TH * GW, DD)
        keep_band = lax.dynamic_slice_in_dim(keep_grid, band_start, TH, 0).reshape(TH * GW)
        pixel_band = lax.dynamic_slice_in_dim(pixels, band_start, TH, 0).reshape(TH * GW, PD).astype(jnp.float32)
        decoded = (inputs_band + jnp.dot(attended, w_out, preferred_element_type=jnp.float32)).astype(jnp.bfloat16)
        predicted = jnp.dot(decoded, w_head, preferred_element_type=jnp.float32)
        centred = pixel_band - lax.optimization_barrier(jnp.mean(pixel_band, axis=1, keepdims=True))
        normalized = centred * lax.rsqrt(lax.optimization_barrier(jnp.mean(centred * centred, axis=1, keepdims=True)) + EPSILON)
        error = (predicted - normalized) * (1.0 - keep_band)[:, None]
        squared = 0.5 * lax.optimization_barrier(jnp.sum((error * error).reshape(TH, N_EXPERT, TW, PD), axis=(0, 2, 3))) / (TILE * PD)
        d_pred = error.astype(jnp.bfloat16)
        back_hidden = jnp.dot(d_pred, w_head.T, preferred_element_type=jnp.float32).astype(jnp.bfloat16)
        d_attn = jnp.dot(back_hidden, w_out.T, preferred_element_type=jnp.float32).astype(jnp.bfloat16)
        return (decoded.reshape(TH, GW, DD), d_attn.reshape(TH, GW, DD), squared)
    decoded, d_attn, tile_loss = lax.map(band_work, jnp.arange(N_DP, dtype=jnp.int32))
    return (decoded.reshape(GH, GW, DD), d_attn.reshape(GH, GW, DD), tile_loss)
```

```python
import functools
import math

import jax
import jax.numpy as jnp
from jax import lax
from jax.experimental import pallas as pl
from jax.experimental.pallas import tpu as pltpu
from jax.sharding import PartitionSpec as P

TOPK = 2
HD = 32
PD = 768
RAD = 3


EPSILON = 1e-06


def padded(value, sides, width):
    for axis, dim in sides:
        count, length = (lax.axis_size(axis), value.shape[dim])
        up = [(i, (i + 1) % count) for i in range(count - 1)]
        down = [(j, i) for i, j in up]
        last = lax.slice_in_dim(value, length - width, length, axis=dim)
        initial = lax.slice_in_dim(value, 0, width, axis=dim)
        before = lax.ppermute(last, axis, up)
        after = lax.ppermute(initial, axis, down)
        value = jnp.concatenate([before, value, after], axis=dim)
    return value


def positional(row_ids, col_ids, total_width):
    quarter = total_width // 4
    frequency = jnp.exp(jnp.arange(quarter, dtype=jnp.float32) * (-math.log(10000.0) / quarter))
    row_angle = row_ids.astype(jnp.float32)[:, None] * frequency[None, :]
    col_angle = col_ids.astype(jnp.float32)[:, None] * frequency[None, :]
    height = row_angle.shape[0]
    breadth = col_angle.shape[0]
    row_part = jnp.broadcast_to(
        jnp.concatenate([jnp.sin(row_angle), jnp.cos(row_angle)], 1)[:, None, :],
        (height, breadth, 2 * quarter),
    )
    col_part = jnp.broadcast_to(
        jnp.concatenate([jnp.sin(col_angle), jnp.cos(col_angle)], 1)[None, :, :],
        (height, breadth, 2 * quarter),
    )
    return jnp.concatenate([row_part, col_part], 2)


def slot_ranks(labels, buckets, slot_width):
    one_hot = (labels[:, None] == jnp.arange(buckets, dtype=jnp.int32)[None, :]).astype(jnp.int32)
    rank_in = jnp.sum((jnp.cumsum(one_hot, axis=0) - 1) * one_hot, axis=1)
    return labels * slot_width + rank_in


def fill_slots(source, slots, slot_total, repeat_count):
    entries = slots.shape[0]
    owner_row = (
        jnp.full((slot_total + 1,), -1, jnp.int32)
        .at[slots]
        .set(jnp.arange(entries, dtype=jnp.int32))[:slot_total]
    )
    taken = source[jnp.maximum(owner_row, 0) // repeat_count]
    return jnp.where((owner_row >= 0)[:, None], taken, jnp.zeros_like(taken))


QH=4; QW=16; KW=24
NEG=-1e30
def dot(a,b,dims=((1,),(0,))):
    return lax.dot_general(a,b,(dims,((),())),preferred_element_type=jnp.float32)

def decoder_kernel(grid_h, grid_w, place_ref, normed_ref, dec_in_ref, keep_ref, pixels_ref, wqkv_ref, wout_ref, whead_ref,
                   decoded_ref, dattn_ref, loss_ref, q_ref, kv_ref, att_ref):
    th, tw, pd = pixels_ref.shape
    rows_p, cols_p, dd = normed_ref.shape
    group = 256
    heads = group // HD
    bf = jnp.bfloat16
    for r in range(rows_p):
        x = normed_ref[r]
        kv = dot(x, wqkv_ref[:, dd:])
        kv_ref[r] = kv.astype(bf).astype(jnp.float32)
    for r in range(th):
        x = normed_ref[r + RAD, :, :].astype(jnp.float32)[RAD:RAD + tw].astype(bf)
        q_ref[r] = dot(x, wqkv_ref[:, :dd]).astype(bf)
    band_row = place_ref[0]
    owner = place_ref[1]
    lane_head = lax.broadcasted_iota(jnp.int32, (1, group), 1) // HD
    head_masks = [(lane_head == h) for h in range(heads)]
    head_ones = [m.astype(jnp.float32).astype(bf) for m in head_masks]
    keys = (QH + 2 * RAD) * KW
    slab = -(-keys // 256) * 256
    qi = lax.broadcasted_iota(jnp.int32, (QH * QW, slab), 0)
    ki = lax.broadcasted_iota(jnp.int32, (QH * QW, slab), 1)
    q_row, q_col = qi // QW, qi % QW
    k_row, k_col = ki // KW, ki % KW
    near = (k_row >= q_row) & (k_row <= q_row + 2 * RAD) & (k_col >= q_col) & (k_col <= q_col + 2 * RAD) & (ki < keys)
    c = math.log2(math.e) / math.sqrt(HD)
    fill = jnp.zeros((slab - keys, group), bf)

    def column(j, carry):
        c0 = pl.multiple_of(j * QW, QW)
        for rt in range(th // QH):
            g_row = band_row * th + rt * QH - RAD + k_row
            g_col = owner * tw + j * QW - RAD + k_col
            ok = near & (g_row >= 0) & (g_row < grid_h) & (g_col >= 0) & (g_col < grid_w)
            bias = jnp.where(ok, 0.0, NEG)
            for g in range(dd // group):
                qt = q_ref[rt * QH:(rt + 1) * QH, pl.ds(c0, QW), g * group:(g + 1) * group].reshape(QH * QW, group)
                ks = kv_ref[rt * QH:rt * QH + QH + 2 * RAD, pl.ds(c0, KW), g * group:(g + 1) * group].reshape(keys, group).astype(bf)
                vs = kv_ref[rt * QH:rt * QH + QH + 2 * RAD, pl.ds(c0, KW), dd + g * group:dd + (g + 1) * group].reshape(keys, group).astype(bf)
                ks = jnp.concatenate([ks, fill], 0)
                vs = jnp.concatenate([vs, fill], 0)
                qx = jnp.concatenate([qt * head_ones[h] for h in range(heads)], 0)
                s = dot(qx, ks, ((1,), (1,)))
                e = jnp.exp2(s.reshape(heads, QH * QW, slab) * c + bias[None]).reshape(heads * QH * QW, slab)
                den = jnp.sum(e, axis=1, keepdims=True)
                o = dot(e.astype(bf), vs)
                o = (o * (1.0 / den)).reshape(heads, QH * QW, group)
                out = jnp.where(head_masks[0], o[0], 0.0)
                for h in range(1, heads):
                    out = jnp.where(head_masks[h], o[h], out)
                att_ref[rt * QH:(rt + 1) * QH, pl.ds(c0, QW), g * group:(g + 1) * group] = out.astype(bf).reshape(QH, QW, group)
        return carry
    lax.fori_loop(0, tw // QW, column, 0)

    loss = jnp.zeros((1, 1), jnp.float32)
    for r in range(th):
        att = att_ref[r]
        decoded = (dec_in_ref[r] + dot(att, wout_ref[...])).astype(bf)
        decoded_ref[r] = decoded
        pred = dot(decoded, whead_ref[...])
        pix = pixels_ref[r].astype(jnp.float32)
        cen = pix - jnp.sum(pix, axis=1, keepdims=True) * (1.0 / pd)
        var = jnp.sum(cen * cen, axis=1, keepdims=True) * (1.0 / pd)
        err = (pred - cen * lax.rsqrt(var + EPSILON)) * (1.0 - keep_ref[r])
        loss = loss + jnp.sum(jnp.sum(err * err, axis=1, keepdims=True), axis=0, keepdims=True)
        back = dot(err.astype(bf), whead_ref[...], ((1,), (1,))).astype(bf)
        dattn_ref[r] = dot(back, wout_ref[...], ((1,), (1,))).astype(bf)
    loss_ref[...] = loss * (0.5 / (th * tw * pd))

def decoder(place, normed_padded, dec_in, keep, pixels, w_qkv, w_out, w_head, grid_h, grid_w):
    th, tw, pd = pixels.shape
    dd = normed_padded.shape[2]
    extra = -(-(tw + KW - QW) // 16) * 16 - normed_padded.shape[1]
    normed_padded = jnp.pad(normed_padded, ((0, 0), (0, extra), (0, 0)))
    cols = normed_padded.shape[1]
    vm = pl.BlockSpec(memory_space=pltpu.VMEM)
    return pl.pallas_call(
        functools.partial(decoder_kernel, grid_h, grid_w),
        out_shape=(jax.ShapeDtypeStruct((th, tw, dd), jnp.bfloat16), jax.ShapeDtypeStruct((th, tw, dd), jnp.bfloat16), jax.ShapeDtypeStruct((1, 1), jnp.float32)),
        in_specs=[pl.BlockSpec(memory_space=pltpu.SMEM)] + [vm] * 7,
        out_specs=(vm, vm, vm),
        scratch_shapes=[pltpu.VMEM((th, tw, dd), jnp.bfloat16), pltpu.VMEM((th + 2 * RAD, cols, 2 * dd), jnp.float32), pltpu.VMEM((th, tw, dd), jnp.bfloat16)],
        compiler_params=pltpu.CompilerParams(vmem_limit_bytes=48 * 2**20),
        name="decoder",
    )(place, normed_padded, dec_in, keep, pixels, w_qkv, w_out, w_head)


def local(
    tokens,
    expert_ids,
    gate_weights,
    target,
    expert_gate,
    expert_up,
    expert_down,
    dec_embed,
    mask_token,
    norm_gain,
    w_qkv,
    w_out,
    w_head,
    pixels,
):
    groups = lax.axis_size("expert")
    tok_rows = tokens.shape[0]
    model_width = tokens.shape[1]
    local_experts = expert_gate.shape[0]
    experts_all = local_experts * groups
    capacity = 3 * tok_rows * TOPK // (2 * experts_all)
    tile_height = pixels.shape[0]
    tile_width = pixels.shape[1]
    tile_size = tile_height * tile_width
    relay_cap = tile_size // groups
    dec_width = dec_embed.shape[1]
    flat_ids = expert_ids.reshape(-1)
    expert_slots = slot_ranks(flat_ids, experts_all, capacity)
    outgoing = fill_slots(tokens, expert_slots, experts_all * capacity, TOPK)
    outgoing = outgoing.reshape(groups, local_experts, capacity, model_width)
    arrived = lax.all_to_all(outgoing, "expert", split_axis=0, concat_axis=0, tiled=True)
    gate_part = jnp.einsum(
        "gecd,edf->gecf", arrived, expert_gate, preferred_element_type=jnp.float32
    )
    up_part = jnp.einsum("gecd,edf->gecf", arrived, expert_up, preferred_element_type=jnp.float32)
    expert_hidden = (jax.nn.silu(gate_part) * up_part).astype(jnp.bfloat16)
    outcome = jnp.einsum(
        "gecf,efd->gecd", expert_hidden, expert_down, preferred_element_type=jnp.float32
    ).astype(jnp.bfloat16)
    returned = lax.all_to_all(outcome, "expert", split_axis=0, concat_axis=0, tiled=True)
    picked = returned.reshape(experts_all * capacity, model_width)[expert_slots].reshape(
        tok_rows, TOPK, model_width
    )
    mixed = tokens.astype(jnp.float32)
    for slot_index in range(TOPK):
        mixed = mixed + gate_weights[:, slot_index, None] * picked[:, slot_index].astype(
            jnp.float32
        )
    moe_out = mixed.astype(jnp.bfloat16)
    tile_of_row = target // tile_size
    relay_slots = slot_ranks(tile_of_row, groups, relay_cap)
    payload = jnp.dot(moe_out, dec_embed, preferred_element_type=jnp.float32).astype(jnp.bfloat16)
    payload_width = payload.shape[1]
    packed = fill_slots(payload, relay_slots, groups * relay_cap, 1)
    landed = lax.all_to_all(
        packed.reshape(groups, relay_cap, payload_width),
        "expert",
        split_axis=0,
        concat_axis=0,
        tiled=True,
    )
    landed = landed.reshape(groups * relay_cap, payload_width)
    every_target = lax.all_gather(target, "expert", axis=0, tiled=True).reshape(groups, tok_rows)
    owner = lax.axis_index("expert")
    band_row = lax.axis_index("dp")
    mine = (every_target // tile_size == owner).astype(jnp.int32)
    rank_mine = jnp.cumsum(mine, axis=1) - 1
    source_ids = jnp.arange(groups, dtype=jnp.int32)[:, None]
    slot_total = groups * relay_cap
    slot_of = jnp.where(mine > 0, source_ids * relay_cap + rank_mine, slot_total)
    spot = jnp.where(mine > 0, every_target % tile_size, tile_size)
    lookup = (
        jnp.full((tile_size + 1,), slot_total, jnp.int32)
        .at[spot.reshape(-1)]
        .set(slot_of.reshape(-1))[:tile_size]
    )
    keep = lookup < slot_total
    visible = landed[jnp.minimum(lookup, slot_total - 1)]
    row_ids = band_row * tile_height + jnp.arange(tile_height, dtype=jnp.int32)
    col_ids = owner * tile_width + jnp.arange(tile_width, dtype=jnp.int32)
    position = positional(row_ids, col_ids, dec_width).reshape(tile_size, dec_width)
    decoder_in = (
        jnp.where(
            keep[:, None], visible.astype(jnp.float32), mask_token.astype(jnp.float32)[None, :]
        )
        + position
    )
    mean_square = jnp.mean(decoder_in * decoder_in, axis=1, keepdims=True)
    normed = (decoder_in * lax.rsqrt(mean_square + EPSILON) * norm_gain[None, :]).astype(
        jnp.bfloat16
    )
    normed_grid = normed.reshape(tile_height, tile_width, dec_width)
    normed_padded = padded(normed_grid, (("dp", 0), ("expert", 1)), RAD)
    place = jnp.stack([band_row, owner]).astype(jnp.int32)
    return decoder(
        place,
        normed_padded,
        decoder_in.reshape(tile_height, tile_width, dec_width),
        keep.astype(jnp.float32).reshape(tile_height, tile_width, 1),
        pixels,
        w_qkv,
        w_out,
        w_head,
        tile_height * lax.axis_size("dp"),
        tile_width * groups,
    )


def solution(mesh):
    in_specs = (
        P(("dp", "expert"), None),
        P(("dp", "expert"), None),
        P(("dp", "expert"), None),
        P(("dp", "expert")),
        P("expert", None, None),
        P("expert", None, None),
        P("expert", None, None),
        P(),
        P(),
        P(),
        P(),
        P(),
        P(),
        P("dp", "expert", None),
    )
    out_specs = (P("dp", "expert", None), P("dp", "expert", None), P("dp", "expert"))
    return jax.shard_map(local, mesh=mesh, in_specs=in_specs, out_specs=out_specs, check_vma=False)
```

```python
import functools
import math

import jax
import jax.numpy as jnp
from jax import lax
from jax.experimental import pallas as pl
from jax.experimental.pallas import tpu as pltpu
from jax.sharding import PartitionSpec as P

TOPK = 2
HD = 32
PD = 768
RAD = 3


EPSILON = 1e-06


def positional(row_ids, col_ids, total_width):
    quarter = total_width // 4
    frequency = jnp.exp(jnp.arange(quarter, dtype=jnp.float32) * (-math.log(10000.0) / quarter))
    row_angle = row_ids.astype(jnp.float32)[:, None] * frequency[None, :]
    col_angle = col_ids.astype(jnp.float32)[:, None] * frequency[None, :]
    return (
        jnp.concatenate([jnp.sin(row_angle), jnp.cos(row_angle)], 1),
        jnp.concatenate([jnp.sin(col_angle), jnp.cos(col_angle)], 1),
    )


def dot(a, b, dims=((1,), (0,))):
    return lax.dot_general(a, b, (dims, ((), ())), preferred_element_type=jnp.float32)


def iota(shape, axis):
    return lax.broadcasted_iota(jnp.int32, shape, axis)


def ones_where(mask):
    return jnp.where(mask, 1.0, 0.0).astype(jnp.bfloat16)


def route_of(width, local_experts, total, axis, shape):
    slot = iota(shape, axis)
    block = slot // (local_experts * width)
    return (block ^ lax.axis_index("expert")) * local_experts + slot // width % local_experts


def slot_matrix(member, width, route):
    buckets, items = member.shape
    total = route.shape[0]
    earlier = ones_where(iota((items, items), 0) < iota((items, items), 1))
    rank = dot(ones_where(member), earlier)
    code = jnp.where(member, rank, -1.0).astype(jnp.bfloat16)
    expand = ones_where(route == iota((total, buckets), 1))
    place = (iota((total, items), 0) % width).astype(jnp.float32)
    return ones_where(dot(expand, code) == place)


def pack_kernel(width, experts, local_experts, ids_ref, tokens_ref, *out_refs):
    items = tokens_ref.shape[0]
    total = experts * width
    member = iota((experts, items), 0) == ids_ref[0:1, :]
    for k in range(1, ids_ref.shape[0]):
        member = member | (iota((experts, items), 0) == ids_ref[k : k + 1, :])
    route = route_of(width, local_experts, total, 0, (total, experts))
    rows = dot(slot_matrix(member, width, route), tokens_ref[...]).astype(jnp.bfloat16)
    share = local_experts * width
    for k, out_ref in enumerate(out_refs):
        out_ref[...] = rows[k * share : (k + 1) * share].reshape(out_ref.shape)


def prep_kernel(
    width, experts, local_experts, relay_cap, tile_size, ids_ref, gates_ref, target_ref, tokens_ref, embed_ref,
    high_ref, low_ref, base_ref, relay_ref, spot_ref,
):
    items = tokens_ref.shape[0]
    slots = high_ref.shape[1]
    lines = iota((experts, items), 0)
    member = jnp.zeros((experts, items), jnp.float32)
    gates = jnp.zeros((experts, items), jnp.float32)
    for k in range(ids_ref.shape[0]):
        hit = ids_ref[k : k + 1, :] == lines
        member = jnp.where(hit, 1.0, member)
        gates = jnp.where(hit, gates_ref[k : k + 1, :], gates)
    earlier = ones_where(iota((items, items), 0) < iota((items, items), 1))
    rank = dot(member.astype(jnp.bfloat16), earlier)
    code = jnp.where(member > 0.5, rank, -1.0).astype(jnp.bfloat16)
    route = route_of(width, local_experts, slots, 1, (experts, slots))
    expand = ones_where(route == iota((experts, slots), 0))
    place = (iota((items, slots), 1) % width).astype(jnp.float32)
    across = ((0,), (0,))
    taken = dot(code, expand, across) == place
    high = gates.astype(jnp.bfloat16)
    low = (gates - high.astype(jnp.float32)).astype(jnp.bfloat16)
    high_ref[...] = jnp.where(taken, dot(high, expand, across), 0.0).astype(jnp.bfloat16)
    low_ref[...] = jnp.where(taken, dot(low, expand, across), 0.0).astype(jnp.bfloat16)
    base_ref[...] = dot(tokens_ref[...], embed_ref[...])
    target = target_ref[...]
    relay_slots = relay_ref.shape[0]
    groups = relay_slots // relay_cap
    me = lax.axis_index("expert")
    route = iota((relay_slots, groups), 0) // relay_cap ^ me
    relay = slot_matrix(iota((groups, items), 0) == target // tile_size, relay_cap, route)
    relay_ref[...] = relay
    spot = target % tile_size
    line = iota((8, items), 0)
    digits = jnp.where(line == 0, spot // 256, jnp.where(line == 1, spot % 256, 1)).astype(jnp.float32)
    found = dot(digits.astype(jnp.bfloat16), relay, ((1,), (1,)))
    spots = jnp.where(found[2:3] > 0.5, found[0:1] * 256.0 + found[1:2], -1.0).astype(jnp.int32)
    for k in range(groups):
        spot_ref[pl.ds(me ^ k, 1), :] = spots[:, k * relay_cap : (k + 1) * relay_cap]


def fold_kernel(down_ref, embed_ref, folded_ref):
    folded_ref[0] = dot(down_ref[0], embed_ref[...]).astype(jnp.bfloat16)


def fold(down, embed):
    local_experts, hidden, model_width = down.shape
    out_width = embed.shape[1]
    chunk = hidden // 2
    return pl.pallas_call(
        fold_kernel,
        grid=(local_experts, hidden // chunk),
        out_shape=shaped((local_experts, hidden, out_width), jnp.bfloat16),
        in_specs=[
            pl.BlockSpec((1, chunk, model_width), lambda e, f: (e, f, 0)),
            pl.BlockSpec((model_width, out_width), lambda e, f: (0, 0)),
        ],
        out_specs=pl.BlockSpec((1, chunk, out_width), lambda e, f: (e, f, 0)),
        compiler_params=pltpu.CompilerParams(vmem_limit_bytes=WIDE_ROOM),
        cost_estimate=pl.CostEstimate(
            flops=2 * local_experts * hidden * model_width * out_width,
            bytes_accessed=2 * math.prod(down.shape),
            transcendentals=0,
        ),
        name="fold",
    )(down, embed)


def ffn_kernel(sources, *refs):
    row_refs, (gate_ref, up_ref, down_ref) = refs[:sources], refs[sources : sources + 3]
    out_refs = refs[sources + 3 :]
    width = row_refs[0].shape[1]
    rows = jnp.concatenate([ref[0] for ref in row_refs], 0)
    gate = dot(rows, gate_ref[0])
    up = dot(rows, up_ref[0])
    hidden = (gate / (1.0 + jnp.exp(-gate)) * up).astype(jnp.bfloat16)
    done = dot(hidden, down_ref[0]).astype(jnp.bfloat16)
    for k, ref in enumerate(out_refs):
        ref[0] = done[k * width : (k + 1) * width]


def combine_kernel(groups, relay_cap, high_ref, low_ref, base_ref, relay_ref, *refs):
    back = jnp.concatenate([ref[...].reshape(-1, ref.shape[-1]) for ref in refs[:groups]], 0)
    embedded = base_ref[...] + dot(high_ref[...], back) + dot(low_ref[...], back)
    packed = dot(relay_ref[...], embedded.astype(jnp.bfloat16)).astype(jnp.bfloat16)
    for k, ref in enumerate(refs[groups:]):
        ref[...] = packed[k * relay_cap : (k + 1) * relay_cap]


def place_kernel(groups, spot_ref, mask_ref, row_ref, col_ref, gain_ref, *refs):
    landed_refs = refs[:groups]
    normed_ref, dec_ref, keep_ref, low_ref, high_ref, first_ref, last_ref = refs[groups:]
    height, breadth, width = normed_ref.shape
    half = width // 2
    me = lax.axis_index("expert")
    spot = jnp.concatenate([spot_ref[pl.ds(me ^ k, 1), :] for k in range(groups)], 1)
    landed = jnp.concatenate([ref[...] for ref in landed_refs], 0)
    slots = landed.shape[0]
    rim = low_ref.shape[0]
    edge = first_ref.shape[1]
    for r in range(height):
        hit = spot == iota((breadth, slots), 0) + r * breadth
        ones = jnp.where(hit, 1.0, 0.0)
        keep = jnp.sum(ones, axis=1, keepdims=True)
        seen = dot(ones.astype(jnp.bfloat16), landed)
        seen = jnp.where(keep > 0.5, seen, mask_ref[...].astype(jnp.float32))
        left = seen[:, :half] + row_ref[r : r + 1, :]
        right = seen[:, half:] + col_ref[...]
        state = jnp.concatenate([left, right], 1)
        square = jnp.sum(state * state, axis=1, keepdims=True) * (1.0 / width)
        normed = (state * lax.rsqrt(square + EPSILON) * gain_ref[...]).astype(jnp.bfloat16)
        normed_ref[r] = normed
        dec_ref[r] = state
        keep_ref[r] = keep
        first_ref[r] = normed[:edge]
        last_ref[r] = normed[breadth - edge :]
        if r < rim:
            low_ref[r] = normed
        if r >= height - rim:
            high_ref[r - height + rim] = normed


VM = pl.BlockSpec(memory_space=pltpu.VMEM)
ROOM = 16 * 2**20
WIDE_ROOM = 56 * 2**20


def whole_call(kernel, outs, ins, name, flops, scratch=(), room=ROOM):
    size = sum(math.prod(a.shape) * a.dtype.itemsize for a in tuple(outs) + tuple(ins))
    return pl.pallas_call(
        kernel,
        out_shape=tuple(outs),
        in_specs=[VM] * len(ins),
        out_specs=tuple([VM] * len(outs)),
        scratch_shapes=list(scratch),
        compiler_params=pltpu.CompilerParams(vmem_limit_bytes=room),
        cost_estimate=pl.CostEstimate(flops=flops, bytes_accessed=size, transcendentals=0),
        name=name,
    )(*ins)


def shaped(shape, dtype):
    return jax.ShapeDtypeStruct(shape, dtype)


def experts_apply(blocks, gate, up, down, name):
    sources = len(blocks)
    local_experts, width, model_width = blocks[0].shape
    hidden = gate.shape[2]
    out_width = down.shape[2]
    each = lambda *shape: pl.BlockSpec((1,) + shape, lambda e: (e, 0, 0))
    return pl.pallas_call(
        functools.partial(ffn_kernel, sources),
        grid=(local_experts,),
        out_shape=[shaped((local_experts, width, out_width), jnp.bfloat16)] * sources,
        in_specs=[each(width, model_width)] * sources
        + [each(model_width, hidden), each(model_width, hidden), each(hidden, out_width)],
        out_specs=[each(width, out_width)] * sources,
        compiler_params=pltpu.CompilerParams(vmem_limit_bytes=WIDE_ROOM),
        cost_estimate=pl.CostEstimate(
            flops=2 * sources * local_experts * width * hidden * (2 * model_width + out_width),
            bytes_accessed=2 * local_experts * hidden * (2 * model_width + out_width),
            transcendentals=0,
        ),
        name=name,
    )(*blocks, gate, up, down)


INNER_ROOM = 32 * 2**20
OUTER_ROOM = 32 * 2**20
SPAN = 32
STRIP = 16


def shift_matrix(cols, total, groups):
    p, q = iota((cols, total), 0), iota((cols, total), 1)
    hit = jnp.zeros((cols, total), jnp.bool_)
    for start, count, origin in groups:
        hit = hit | ((p >= start) & (p < start + count) & (q - origin == p - start))
    return ones_where(hit)


def attention(q_ref, kv_ref, att_ref, starts, first_row, grid_h, grid_w, tile_h, tile_w):
    width = q_ref.shape[2]
    lanes = 256
    heads = lanes // HD
    lane_head = iota((1, lanes), 1) // HD
    masks = [lane_head == h for h in range(heads)]
    picks = [ones_where(m) for m in masks]
    key_rows = 2 + 2 * RAD
    keys = key_rows * SPAN
    scale = math.log2(math.e) / math.sqrt(HD)
    band_row = lax.axis_index("dp")
    owner = lax.axis_index("expert")

    def column(j, carry):
        c0 = pl.multiple_of(j * STRIP, STRIP)
        for count, q_row, k_row in starts:
            items = count * STRIP
            qi, ki = iota((items, keys), 0), iota((items, keys), 1)
            key_row = first_row + k_row + ki // SPAN
            down = key_row - q_row - qi // STRIP
            across = ki % SPAN - qi % STRIP
            grid_row = band_row * tile_h + key_row
            grid_col = owner * tile_w + j * STRIP - RAD + ki % SPAN
            ok = (down >= -RAD) & (down <= RAD) & (across >= 0) & (across <= 2 * RAD)
            ok = ok & (grid_row >= 0) & (grid_row < grid_h) & (grid_col >= 0) & (grid_col < grid_w)
            bias = jnp.where(ok, 0.0, -1e30)
            for g in range(width // lanes):
                part = slice(g * lanes, (g + 1) * lanes)
                queries = q_ref[q_row : q_row + count, pl.ds(c0, STRIP), part].reshape(items, lanes)
                key = kv_ref[k_row : k_row + key_rows, pl.ds(c0, SPAN), part].reshape(keys, lanes)
                value = kv_ref[
                    k_row : k_row + key_rows, pl.ds(c0, SPAN), width + g * lanes : width + (g + 1) * lanes
                ].reshape(keys, lanes)
                stacked = jnp.concatenate([queries * pick for pick in picks], 0)
                score = dot(stacked, key, ((1,), (1,))).reshape(heads, items, keys)
                weight = jnp.exp2(score * scale + bias[None]).reshape(heads * items, keys)
                total = jnp.sum(weight, axis=1, keepdims=True)
                mixed = dot(weight.astype(jnp.bfloat16), value) * (1.0 / total)
                mixed = mixed.reshape(heads, items, lanes)
                out = mixed[0]
                for h in range(1, heads):
                    out = jnp.where(masks[h], mixed[h], out)
                att_ref[q_row : q_row + count, pl.ds(c0, STRIP), part] = out.astype(jnp.bfloat16).reshape(
                    count, STRIP, lanes
                )
        return carry

    lax.fori_loop(0, tile_w // STRIP, column, 0)


def row_groups(rows):
    return [(min(2, rows.stop - r), r) for r in range(rows.start, rows.stop, 2)]


def inner_kernel(grid_h, grid_w, normed_ref, before_ref, after_ref, wqkv_ref, q_ref, kv_ref, att_ref):
    height, breadth, width = normed_ref.shape
    cols = kv_ref.shape[1]
    edge = before_ref.shape[1]
    shift = shift_matrix(
        cols, breadth + 2 * edge, ((RAD, breadth, 0), (0, RAD, breadth + edge - RAD), (RAD + breadth, RAD, breadth + edge))
    )
    rows = []
    for r in range(height):
        joined = jnp.concatenate([normed_ref[r], before_ref[r], after_ref[r]], 0)
        rows.append(dot(shift, joined).astype(jnp.bfloat16))
    wide = jnp.concatenate(rows, 0)
    kv_ref[...] = dot(wide, wqkv_ref[:, width:]).astype(jnp.bfloat16).reshape(kv_ref.shape)
    flat = normed_ref[...].reshape(height * breadth, width)
    q_ref[...] = dot(flat, wqkv_ref[:, :width]).astype(jnp.bfloat16).reshape(q_ref.shape)
    starts = [(n, r, r - RAD) for n, r in row_groups(slice(RAD, height - RAD))]
    attention(q_ref, kv_ref, att_ref, starts, 0, grid_h, grid_w, height, breadth)


def outer_kernel(
    grid_h, grid_w, up_ref, up_edge_ref, down_ref, down_edge_ref, q_ref, kv_in_ref, att_in_ref, dec_in_ref, keep_ref,
    pixels_ref, wqkv_ref, wout_ref, whead_ref, decoded_ref, dattn_ref, loss_ref, kv_ref, att_ref,
):
    height, breadth, pd = pixels_ref.shape
    width = q_ref.shape[2]
    cols = kv_ref.shape[1]
    edge = up_edge_ref.shape[1]
    middle = edge // 2
    bf16 = jnp.bfloat16
    shift = shift_matrix(
        cols, breadth + edge, ((RAD, breadth, 0), (0, RAD, breadth + middle - RAD), (RAD + breadth, RAD, breadth + middle))
    )
    kv_ref[RAD : RAD + height] = kv_in_ref[...]
    for main, side, start in ((up_ref, up_edge_ref, 0), (down_ref, down_edge_ref, RAD + height)):
        wide = [dot(shift, jnp.concatenate([main[r], side[r]], 0)).astype(bf16) for r in range(RAD)]
        kv = dot(jnp.concatenate(wide, 0), wqkv_ref[:, width:]).astype(bf16)
        kv_ref[start : start + RAD] = kv.reshape(RAD, cols, 2 * width)
    inner = slice(RAD, height - RAD)
    att_ref[inner] = att_in_ref[inner]
    starts = [(n, r, r) for n, r in row_groups(slice(0, RAD))]
    starts += [(n, r, min(r, height + 2 * RAD - 2 - 2 * RAD)) for n, r in row_groups(slice(height - RAD, height))]
    attention(q_ref, kv_ref, att_ref, starts, -RAD, grid_h, grid_w, height, breadth)
    loss = jnp.zeros((1, 1), jnp.float32)
    step = height // 2
    for r in range(0, height, step):
        rows = slice(r, r + step)
        count = step * breadth
        att = att_ref[rows].reshape(count, width)
        decoded = (dec_in_ref[rows].reshape(count, width) + dot(att, wout_ref[...])).astype(bf16)
        decoded_ref[rows] = decoded.reshape(step, breadth, width)
        pred = dot(decoded, whead_ref[...])
        pix = pixels_ref[rows].reshape(count, pd).astype(jnp.float32)
        centred = pix - jnp.sum(pix, axis=1, keepdims=True) * (1.0 / pd)
        spread = jnp.sum(centred * centred, axis=1, keepdims=True) * (1.0 / pd)
        error = (pred - centred * lax.rsqrt(spread + EPSILON)) * (1.0 - keep_ref[rows].reshape(count, 1))
        loss = loss + jnp.sum(jnp.sum(error * error, axis=1, keepdims=True), axis=0, keepdims=True)
        back = dot(error.astype(bf16), whead_ref[...], ((1,), (1,))).astype(bf16)
        dattn_ref[rows] = dot(back, wout_ref[...], ((1,), (1,))).astype(bf16).reshape(step, breadth, width)
    loss_ref[...] = loss * (0.5 / (height * breadth * pd))


def local(
    tokens,
    expert_ids,
    gate_weights,
    target,
    expert_gate,
    expert_up,
    expert_down,
    dec_embed,
    mask_token,
    norm_gain,
    w_qkv,
    w_out,
    w_head,
    pixels,
):
    groups = lax.axis_size("expert")
    tok_rows = tokens.shape[0]
    model_width = tokens.shape[1]
    local_experts = expert_gate.shape[0]
    experts_all = local_experts * groups
    capacity = 3 * tok_rows * TOPK // (2 * experts_all)
    tile_height = pixels.shape[0]
    tile_width = pixels.shape[1]
    tile_size = tile_height * tile_width
    relay_cap = tile_size // groups
    dec_width = dec_embed.shape[1]
    bf16 = jnp.bfloat16
    width = -(-capacity // 16) * 16
    slots = experts_all * width
    block = shaped((local_experts, width, model_width), bf16)

    def swap(value, k):
        return value if k == 0 else lax.ppermute(value, "expert", [(i, i ^ k) for i in range(groups)])

    def swap_all(values):
        moved = {k: swap(values[k], k) for k in list(range(cut, groups)) + list(range(cut))[::-1]}
        return [moved[k] for k in range(groups)]

    cut = groups * 3 // 4
    outgoing = whole_call(
        functools.partial(pack_kernel, width, experts_all, local_experts),
        [block] * groups,
        [expert_ids.T, tokens],
        "pack",
        2 * slots * tok_rows * model_width,
        room=WIDE_ROOM,
    )
    outgoing, ids_later, tokens_later, down_later = lax.optimization_barrier(
        (outgoing, expert_ids, tokens, expert_down)
    )
    arrived = swap_all(outgoing)
    relay_slots = groups * relay_cap
    high, low, base, relay, spots = whole_call(
        functools.partial(prep_kernel, width, experts_all, local_experts, relay_cap, tile_size),
        [
            shaped((tok_rows, slots), bf16),
            shaped((tok_rows, slots), bf16),
            shaped((tok_rows, dec_width), jnp.float32),
            shaped((relay_slots, tok_rows), bf16),
            shaped((groups, relay_cap), jnp.int32),
        ],
        [ids_later.T, gate_weights.T, target.reshape(1, tok_rows), tokens_later, dec_embed],
        "prep",
        2 * tok_rows * dec_width * model_width,
        room=WIDE_ROOM,
    )
    spots = lax.all_to_all(spots, "expert", split_axis=0, concat_axis=0, tiled=True)
    folded = fold(down_later, dec_embed)
    arrived, high, low, base, relay, folded, spots = lax.optimization_barrier(
        (arrived, high, low, base, relay, folded, spots)
    )
    returned = swap_all(experts_apply(arrived, expert_gate, expert_up, folded, "experts"))
    packed = whole_call(
        functools.partial(combine_kernel, groups, relay_cap),
        [shaped((relay_cap, dec_width), bf16)] * groups,
        [high, low, base, relay] + returned,
        "combine",
        2 * tok_rows * dec_width * (2 * slots + relay_slots),
    )
    landed = swap_all(packed)
    owner = lax.axis_index("expert")
    band_row = lax.axis_index("dp")
    row_ids = band_row * tile_height + jnp.arange(tile_height, dtype=jnp.int32)
    col_ids = owner * tile_width + jnp.arange(tile_width, dtype=jnp.int32)
    row_table, col_table = positional(row_ids, col_ids, dec_width)
    edge = 16
    grid_shape = (tile_height, tile_width, dec_width)
    normed, decoder_in, keep, top, bottom, first, last = whole_call(
        functools.partial(place_kernel, groups),
        [
            shaped(grid_shape, bf16),
            shaped(grid_shape, jnp.float32),
            shaped((tile_height, tile_width, 1), jnp.float32),
            shaped((RAD, tile_width, dec_width), bf16),
            shaped((RAD, tile_width, dec_width), bf16),
            shaped((tile_height, edge, dec_width), bf16),
            shaped((tile_height, edge, dec_width), bf16),
        ],
        [spots, mask_token.reshape(1, dec_width), row_table, col_table, norm_gain.reshape(1, dec_width)] + landed,
        "place",
        2 * tile_size * relay_slots * dec_width,
    )
    bands = lax.axis_size("dp")
    upward = [(i + 1, i) for i in range(bands - 1)]
    downward = [(i, i + 1) for i in range(bands - 1)]
    above = lax.ppermute(bottom, "dp", downward)
    below = lax.ppermute(top, "dp", upward)
    before = lax.ppermute(last, "expert", [(i, i + 1) for i in range(groups - 1)])
    after = lax.ppermute(first, "expert", [(i + 1, i) for i in range(groups - 1)])
    sides = jnp.concatenate([before[:, edge // 2 :], after[:, : edge // 2]], 1)
    above_edge = lax.ppermute(sides[tile_height - RAD :], "dp", [(i, (i + 1) % bands) for i in range(bands)])
    below_edge = lax.ppermute(sides[:RAD], "dp", [((i + 1) % bands, i) for i in range(bands)])
    grid_height = tile_height * bands
    grid_width = tile_width * groups
    cols = -(-(tile_width - STRIP + SPAN) // 16) * 16
    queries, kv, attended = whole_call(
        functools.partial(inner_kernel, grid_height, grid_width),
        [
            shaped(grid_shape, bf16),
            shaped((tile_height, cols, 2 * dec_width), bf16),
            shaped(grid_shape, bf16),
        ],
        [normed, before, after, w_qkv],
        "inner",
        6 * tile_size * dec_width * dec_width,
        room=INNER_ROOM,
    )
    return whole_call(
        functools.partial(outer_kernel, grid_height, grid_width),
        [shaped(grid_shape, bf16), shaped(grid_shape, bf16), shaped((1, 1), jnp.float32)],
        [above, above_edge, below, below_edge, queries, kv, attended, decoder_in, keep, pixels, w_qkv, w_out, w_head],
        "outer",
        12 * tile_size * dec_width * dec_width,
        [
            pltpu.VMEM((tile_height + 2 * RAD, cols, 2 * dec_width), bf16),
            pltpu.VMEM(grid_shape, bf16),
        ],
        room=OUTER_ROOM,
    )

def solution(mesh):
    in_specs = (
        P(("dp", "expert"), None),
        P(("dp", "expert"), None),
        P(("dp", "expert"), None),
        P(("dp", "expert")),
        P("expert", None, None),
        P("expert", None, None),
        P("expert", None, None),
        P(),
        P(),
        P(),
        P(),
        P(),
        P(),
        P("dp", "expert", None),
    )
    out_specs = (P("dp", "expert", None), P("dp", "expert", None), P("dp", "expert"))
    return jax.shard_map(local, mesh=mesh, in_specs=in_specs, out_specs=out_specs, check_vma=False)
```

```python
import functools
import math

import jax
import jax.numpy as jnp
from jax import lax
from jax.experimental import pallas as pl
from jax.experimental.pallas import tpu as pltpu
from jax.sharding import PartitionSpec as P

TOPK = 2
HD = 32
PD = 768
RAD = 3


EPSILON = 1e-06


def positional(row_ids, col_ids, total_width):
    quarter = total_width // 4
    frequency = jnp.exp(jnp.arange(quarter, dtype=jnp.float32) * (-math.log(10000.0) / quarter))
    row_angle = row_ids.astype(jnp.float32)[:, None] * frequency[None, :]
    col_angle = col_ids.astype(jnp.float32)[:, None] * frequency[None, :]
    return (
        jnp.concatenate([jnp.sin(row_angle), jnp.cos(row_angle)], 1),
        jnp.concatenate([jnp.sin(col_angle), jnp.cos(col_angle)], 1),
    )


def dot(a, b, dims=((1,), (0,))):
    return lax.dot_general(a, b, (dims, ((), ())), preferred_element_type=jnp.float32)


def iota(shape, axis):
    return lax.broadcasted_iota(jnp.int32, shape, axis)


def ones_where(mask):
    return jnp.where(mask, 1.0, 0.0).astype(jnp.bfloat16)


def route_of(width, local_experts, total, axis, shape):
    slot = iota(shape, axis)
    block = slot // (local_experts * width)
    return (block ^ lax.axis_index("expert")) * local_experts + slot // width % local_experts


def slot_matrix(member, width, route):
    buckets, items = member.shape
    total = route.shape[0]
    earlier = ones_where(iota((items, items), 0) < iota((items, items), 1))
    rank = dot(ones_where(member), earlier)
    code = jnp.where(member, rank, -1.0).astype(jnp.bfloat16)
    expand = ones_where(route == iota((total, buckets), 1))
    place = (iota((total, items), 0) % width).astype(jnp.float32)
    return ones_where(dot(expand, code) == place)


def pack_kernel(width, experts, local_experts, ids_ref, tokens_ref, *out_refs):
    items = tokens_ref.shape[0]
    total = experts * width
    member = iota((experts, items), 0) == ids_ref[0:1, :]
    for k in range(1, ids_ref.shape[0]):
        member = member | (iota((experts, items), 0) == ids_ref[k : k + 1, :])
    route = route_of(width, local_experts, total, 0, (total, experts))
    rows = dot(slot_matrix(member, width, route), tokens_ref[...]).astype(jnp.bfloat16)
    share = local_experts * width
    for k, out_ref in enumerate(out_refs):
        out_ref[...] = rows[k * share : (k + 1) * share].reshape(out_ref.shape)


def prep_kernel(
    width, experts, local_experts, relay_cap, tile_size, ids_ref, gates_ref, target_ref, tokens_ref, embed_ref,
    high_ref, low_ref, base_ref, relay_ref, spot_ref,
):
    items = tokens_ref.shape[0]
    slots = high_ref.shape[1]
    lines = iota((experts, items), 0)
    member = jnp.zeros((experts, items), jnp.float32)
    gates = jnp.zeros((experts, items), jnp.float32)
    for k in range(ids_ref.shape[0]):
        hit = ids_ref[k : k + 1, :] == lines
        member = jnp.where(hit, 1.0, member)
        gates = jnp.where(hit, gates_ref[k : k + 1, :], gates)
    earlier = ones_where(iota((items, items), 0) < iota((items, items), 1))
    rank = dot(member.astype(jnp.bfloat16), earlier)
    code = jnp.where(member > 0.5, rank, -1.0).astype(jnp.bfloat16)
    route = route_of(width, local_experts, slots, 1, (experts, slots))
    expand = ones_where(route == iota((experts, slots), 0))
    place = (iota((items, slots), 1) % width).astype(jnp.float32)
    across = ((0,), (0,))
    taken = dot(code, expand, across) == place
    high = gates.astype(jnp.bfloat16)
    low = (gates - high.astype(jnp.float32)).astype(jnp.bfloat16)
    high_ref[...] = jnp.where(taken, dot(high, expand, across), 0.0).astype(jnp.bfloat16)
    low_ref[...] = jnp.where(taken, dot(low, expand, across), 0.0).astype(jnp.bfloat16)
    base_ref[...] = dot(tokens_ref[...], embed_ref[...])
    target = target_ref[...]
    relay_slots = relay_ref.shape[0]
    groups = relay_slots // relay_cap
    me = lax.axis_index("expert")
    route = iota((relay_slots, groups), 0) // relay_cap ^ me
    relay = slot_matrix(iota((groups, items), 0) == target // tile_size, relay_cap, route)
    relay_ref[...] = relay
    spot = target % tile_size
    line = iota((8, items), 0)
    digits = jnp.where(line == 0, spot // 256, jnp.where(line == 1, spot % 256, 1)).astype(jnp.float32)
    found = dot(digits.astype(jnp.bfloat16), relay, ((1,), (1,)))
    spots = jnp.where(found[2:3] > 0.5, found[0:1] * 256.0 + found[1:2], -1.0).astype(jnp.int32)
    for k in range(groups):
        spot_ref[pl.ds(me ^ k, 1), :] = spots[:, k * relay_cap : (k + 1) * relay_cap]


def fold_kernel(down_ref, embed_ref, folded_ref):
    folded_ref[0] = dot(down_ref[0], embed_ref[...]).astype(jnp.bfloat16)


def fold(down, embed):
    local_experts, hidden, model_width = down.shape
    out_width = embed.shape[1]
    chunk = hidden // 2
    return pl.pallas_call(
        fold_kernel,
        grid=(local_experts, hidden // chunk),
        out_shape=shaped((local_experts, hidden, out_width), jnp.bfloat16),
        in_specs=[
            pl.BlockSpec((1, chunk, model_width), lambda e, f: (e, f, 0)),
            pl.BlockSpec((model_width, out_width), lambda e, f: (0, 0)),
        ],
        out_specs=pl.BlockSpec((1, chunk, out_width), lambda e, f: (e, f, 0)),
        compiler_params=pltpu.CompilerParams(vmem_limit_bytes=WIDE_ROOM),
        cost_estimate=pl.CostEstimate(
            flops=2 * local_experts * hidden * model_width * out_width,
            bytes_accessed=2 * math.prod(down.shape),
            transcendentals=0,
        ),
        name="fold",
    )(down, embed)


def ffn_kernel(sources, *refs):
    row_refs, (gate_ref, up_ref, down_ref) = refs[:sources], refs[sources : sources + 3]
    out_refs = refs[sources + 3 :]
    width = row_refs[0].shape[1]
    rows = jnp.concatenate([ref[0] for ref in row_refs], 0)
    gate = dot(rows, gate_ref[0])
    up = dot(rows, up_ref[0])
    hidden = (gate / (1.0 + jnp.exp(-gate)) * up).astype(jnp.bfloat16)
    done = dot(hidden, down_ref[0]).astype(jnp.bfloat16)
    for k, ref in enumerate(out_refs):
        ref[0] = done[k * width : (k + 1) * width]


def combine_kernel(groups, relay_cap, high_ref, low_ref, base_ref, relay_ref, *refs):
    back = jnp.concatenate([ref[...].reshape(-1, ref.shape[-1]) for ref in refs[:groups]], 0)
    embedded = base_ref[...] + dot(high_ref[...], back) + dot(low_ref[...], back)
    packed = dot(relay_ref[...], embedded.astype(jnp.bfloat16)).astype(jnp.bfloat16)
    for k, ref in enumerate(refs[groups:]):
        ref[...] = packed[k * relay_cap : (k + 1) * relay_cap]


def place_kernel(groups, spot_ref, mask_ref, row_ref, col_ref, gain_ref, *refs):
    landed_refs = refs[:groups]
    normed_ref, dec_ref, keep_ref, low_ref, high_ref, first_ref, last_ref = refs[groups:]
    height, breadth, width = normed_ref.shape
    half = width // 2
    me = lax.axis_index("expert")
    spot = jnp.concatenate([spot_ref[pl.ds(me ^ k, 1), :] for k in range(groups)], 1)
    landed = jnp.concatenate([ref[...] for ref in landed_refs], 0)
    slots = landed.shape[0]
    rim = low_ref.shape[0]
    edge = first_ref.shape[1]
    for r in range(height):
        hit = spot == iota((breadth, slots), 0) + r * breadth
        ones = jnp.where(hit, 1.0, 0.0)
        keep = jnp.sum(ones, axis=1, keepdims=True)
        seen = dot(ones.astype(jnp.bfloat16), landed)
        seen = jnp.where(keep > 0.5, seen, mask_ref[...].astype(jnp.float32))
        left = seen[:, :half] + row_ref[r : r + 1, :]
        right = seen[:, half:] + col_ref[...]
        state = jnp.concatenate([left, right], 1)
        square = jnp.sum(state * state, axis=1, keepdims=True) * (1.0 / width)
        normed = (state * lax.rsqrt(square + EPSILON) * gain_ref[...]).astype(jnp.bfloat16)
        normed_ref[r] = normed
        dec_ref[r] = state
        keep_ref[r] = keep
        first_ref[r] = normed[:edge]
        last_ref[r] = normed[breadth - edge :]
        if r < rim:
            low_ref[r] = normed
        if r >= height - rim:
            high_ref[r - height + rim] = normed


VM = pl.BlockSpec(memory_space=pltpu.VMEM)
ROOM = 16 * 2**20
WIDE_ROOM = 56 * 2**20


def whole_call(kernel, outs, ins, name, flops, scratch=(), room=ROOM, last=VM):
    size = sum(math.prod(a.shape) * a.dtype.itemsize for a in tuple(outs) + tuple(ins))
    return pl.pallas_call(
        kernel,
        out_shape=tuple(outs),
        in_specs=[VM] * (len(ins) - 1) + [last],
        out_specs=tuple([VM] * len(outs)),
        scratch_shapes=list(scratch),
        compiler_params=pltpu.CompilerParams(vmem_limit_bytes=room),
        cost_estimate=pl.CostEstimate(flops=flops, bytes_accessed=size, transcendentals=0),
        name=name,
    )(*ins)


def shaped(shape, dtype):
    return jax.ShapeDtypeStruct(shape, dtype)


def experts_apply(blocks, gate, up, down, name):
    sources = len(blocks)
    local_experts, width, model_width = blocks[0].shape
    hidden = gate.shape[2]
    out_width = down.shape[2]
    each = lambda *shape: pl.BlockSpec((1,) + shape, lambda e: (e, 0, 0))
    return pl.pallas_call(
        functools.partial(ffn_kernel, sources),
        grid=(local_experts,),
        out_shape=[shaped((local_experts, width, out_width), jnp.bfloat16)] * sources,
        in_specs=[each(width, model_width)] * sources
        + [each(model_width, hidden), each(model_width, hidden), each(hidden, out_width)],
        out_specs=[each(width, out_width)] * sources,
        compiler_params=pltpu.CompilerParams(vmem_limit_bytes=WIDE_ROOM),
        cost_estimate=pl.CostEstimate(
            flops=2 * sources * local_experts * width * hidden * (2 * model_width + out_width),
            bytes_accessed=2 * local_experts * hidden * (2 * model_width + out_width),
            transcendentals=0,
        ),
        name=name,
    )(*blocks, gate, up, down)


INNER_ROOM = 32 * 2**20
OUTER_ROOM = 32 * 2**20
SPAN = 32
STRIP = 16


def shift_matrix(cols, total, groups):
    p, q = iota((cols, total), 0), iota((cols, total), 1)
    hit = jnp.zeros((cols, total), jnp.bool_)
    for start, count, origin in groups:
        hit = hit | ((p >= start) & (p < start + count) & (q - origin == p - start))
    return ones_where(hit)


def attention(q_ref, kv_ref, att_ref, starts, first_row, grid_h, grid_w, tile_h, tile_w):
    width = q_ref.shape[2]
    lanes = 256
    heads = lanes // HD
    lane_head = iota((1, lanes), 1) // HD
    masks = [lane_head == h for h in range(heads)]
    picks = [ones_where(m) for m in masks]
    key_rows = 2 + 2 * RAD
    keys = key_rows * SPAN
    scale = math.log2(math.e) / math.sqrt(HD)
    band_row = lax.axis_index("dp")
    owner = lax.axis_index("expert")

    near = {}
    for count, q_row, k_row in starts:
        qi, ki = iota((count * STRIP, keys), 0), iota((count * STRIP, keys), 1)
        down = ki // SPAN + first_row + k_row - q_row - qi // STRIP
        across = ki % SPAN - qi % STRIP
        ok = (down >= -RAD) & (down <= RAD) & (across >= 0) & (across <= 2 * RAD)
        near[count, k_row - q_row] = ok, ki // SPAN, ki % SPAN
    for j in range(tile_w // STRIP):
        c0 = j * STRIP
        for count, q_row, k_row in starts:
            items = count * STRIP
            ok, key_row, key_col = near[count, k_row - q_row]
            grid_row = band_row * tile_h + first_row + k_row + key_row
            grid_col = owner * tile_w + j * STRIP - RAD + key_col
            ok = ok & (grid_row >= 0) & (grid_row < grid_h) & (grid_col >= 0) & (grid_col < grid_w)
            bias = jnp.where(ok, 0.0, -1e30)
            for g in range(width // lanes):
                part = slice(g * lanes, (g + 1) * lanes)
                queries = q_ref[q_row : q_row + count, pl.ds(c0, STRIP), part].reshape(items, lanes)
                key = kv_ref[k_row : k_row + key_rows, pl.ds(c0, SPAN), part].reshape(keys, lanes)
                value = kv_ref[
                    k_row : k_row + key_rows, pl.ds(c0, SPAN), width + g * lanes : width + (g + 1) * lanes
                ].reshape(keys, lanes)
                stacked = jnp.concatenate([queries * pick for pick in picks], 0)
                score = dot(stacked, key, ((1,), (1,))).reshape(heads, items, keys)
                weight = jnp.exp2(score * scale + bias[None]).reshape(heads * items, keys)
                total = jnp.sum(weight, axis=1, keepdims=True)
                mixed = dot(weight.astype(jnp.bfloat16), value) * (1.0 / total)
                mixed = mixed.reshape(heads, items, lanes)
                out = mixed[0]
                for h in range(1, heads):
                    out = jnp.where(masks[h], mixed[h], out)
                att_ref[q_row : q_row + count, pl.ds(c0, STRIP), part] = out.astype(jnp.bfloat16).reshape(
                    count, STRIP, lanes
                )


def row_groups(rows):
    return [(min(2, rows.stop - r), r) for r in range(rows.start, rows.stop, 2)]


def finish(rows, att_ref, dec_in_ref, keep_ref, pixels_ref, wout_ref, whead_ref, decoded_ref, dattn_ref, offset):
    breadth, width = att_ref.shape[1:]
    pd = pixels_ref.shape[2]
    bf16 = jnp.bfloat16
    lines = rows.stop - rows.start
    count = lines * breadth
    held = slice(rows.start - offset, rows.stop - offset)
    att = att_ref[rows].reshape(count, width)
    decoded = (dec_in_ref[rows].reshape(count, width) + dot(att, wout_ref[...])).astype(bf16)
    decoded_ref[held] = decoded.reshape(lines, breadth, width)
    pred = dot(decoded, whead_ref[...])
    pix = pixels_ref[held].reshape(count, pd).astype(jnp.float32)
    centred = pix - jnp.sum(pix, axis=1, keepdims=True) * (1.0 / pd)
    spread = jnp.sum(centred * centred, axis=1, keepdims=True) * (1.0 / pd)
    error = (pred - centred * lax.rsqrt(spread + EPSILON)) * (1.0 - keep_ref[rows].reshape(count, 1))
    back = dot(error.astype(bf16), whead_ref[...], ((1,), (1,))).astype(bf16)
    dattn_ref[held] = dot(back, wout_ref[...], ((1,), (1,))).astype(bf16).reshape(lines, breadth, width)
    return jnp.sum(jnp.sum(error * error, axis=1, keepdims=True), axis=0, keepdims=True)


def inner_kernel(
    grid_h, grid_w, normed_ref, before_ref, after_ref, dec_in_ref, keep_ref, wqkv_ref, wout_ref, whead_ref, pixels_ref,
    q_ref, kv_ref, decoded_ref, dattn_ref, loss_ref, att_ref, held_ref, sem,
):
    height, breadth, width = normed_ref.shape
    cols = kv_ref.shape[1]
    edge = before_ref.shape[1]
    inner = slice(RAD, height - RAD)
    copy = pltpu.make_async_copy(pixels_ref.at[inner], held_ref, sem)
    copy.start()
    shift = shift_matrix(
        cols, breadth + 2 * edge, ((RAD, breadth, 0), (0, RAD, breadth + edge - RAD), (RAD + breadth, RAD, breadth + edge))
    )
    rows = []
    for r in range(height):
        joined = jnp.concatenate([normed_ref[r], before_ref[r], after_ref[r]], 0)
        rows.append(dot(shift, joined).astype(jnp.bfloat16))
    wide = jnp.concatenate(rows, 0)
    kv_ref[...] = dot(wide, wqkv_ref[:, width:]).astype(jnp.bfloat16).reshape(kv_ref.shape)
    flat = normed_ref[...].reshape(height * breadth, width)
    q_ref[...] = dot(flat, wqkv_ref[:, :width]).astype(jnp.bfloat16).reshape(q_ref.shape)
    starts = [(n, r, r - RAD) for n, r in row_groups(inner)]
    attention(q_ref, kv_ref, att_ref, starts, 0, grid_h, grid_w, height, breadth)
    copy.wait()
    loss_ref[...] = finish(
        inner, att_ref, dec_in_ref, keep_ref, held_ref, wout_ref, whead_ref, decoded_ref, dattn_ref, RAD
    )


def outer_kernel(
    grid_h, grid_w, up_ref, down_ref, q_ref, kv_in_ref, decoded_in_ref, dattn_in_ref, loss_in_ref,
    dec_in_ref, keep_ref, pixels_ref, wqkv_ref, wout_ref, whead_ref, decoded_ref, dattn_ref, loss_ref, kv_ref, att_ref,
):
    height, breadth, pd = pixels_ref.shape
    width = q_ref.shape[2]
    cols = kv_ref.shape[1]
    edge = up_ref.shape[1] - breadth
    middle = edge // 2
    bf16 = jnp.bfloat16
    shift = shift_matrix(
        cols, breadth + edge, ((RAD, breadth, 0), (0, RAD, breadth + middle - RAD), (RAD + breadth, RAD, breadth + middle))
    )
    kv_ref[RAD : RAD + height] = kv_in_ref[...]
    for rim_ref, start in ((up_ref, 0), (down_ref, RAD + height)):
        wide = [dot(shift, rim_ref[r]).astype(bf16) for r in range(RAD)]
        kv = dot(jnp.concatenate(wide, 0), wqkv_ref[:, width:]).astype(bf16)
        kv_ref[start : start + RAD] = kv.reshape(RAD, cols, 2 * width)
    inner = slice(RAD, height - RAD)
    decoded_ref[inner] = decoded_in_ref[...]
    dattn_ref[inner] = dattn_in_ref[...]
    starts = [(2, r, r) for r in range(0, height, 2)]
    attention(q_ref, kv_ref, att_ref, starts, -RAD, grid_h, grid_w, height, breadth)
    loss = loss_in_ref[...]
    for rows in (slice(0, RAD), slice(height - RAD, height)):
        loss = loss + finish(
            rows, att_ref, dec_in_ref, keep_ref, pixels_ref, wout_ref, whead_ref, decoded_ref, dattn_ref, 0
        )
    loss_ref[...] = loss * (0.5 / (height * breadth * pd))


def local(
    tokens,
    expert_ids,
    gate_weights,
    target,
    expert_gate,
    expert_up,
    expert_down,
    dec_embed,
    mask_token,
    norm_gain,
    w_qkv,
    w_out,
    w_head,
    pixels,
):
    groups = lax.axis_size("expert")
    tok_rows = tokens.shape[0]
    model_width = tokens.shape[1]
    local_experts = expert_gate.shape[0]
    experts_all = local_experts * groups
    capacity = 3 * tok_rows * TOPK // (2 * experts_all)
    tile_height = pixels.shape[0]
    tile_width = pixels.shape[1]
    tile_size = tile_height * tile_width
    relay_cap = tile_size // groups
    dec_width = dec_embed.shape[1]
    bf16 = jnp.bfloat16
    width = -(-capacity // 16) * 16
    slots = experts_all * width
    block = shaped((local_experts, width, model_width), bf16)

    def swap(value, k):
        return value if k == 0 else lax.ppermute(value, "expert", [(i, i ^ k) for i in range(groups)])

    def swap_all(values):
        moved = {k: swap(values[k], k) for k in list(range(cut, groups)) + list(range(cut))[::-1]}
        return [moved[k] for k in range(groups)]

    cut = groups * 3 // 4
    outgoing = whole_call(
        functools.partial(pack_kernel, width, experts_all, local_experts),
        [block] * groups,
        [expert_ids.T, tokens],
        "pack",
        2 * slots * tok_rows * model_width,
        room=WIDE_ROOM,
    )
    outgoing, ids_later, tokens_later, down_later = lax.optimization_barrier(
        (outgoing, expert_ids, tokens, expert_down)
    )
    arrived = swap_all(outgoing)
    relay_slots = groups * relay_cap
    high, low, base, relay, spots = whole_call(
        functools.partial(prep_kernel, width, experts_all, local_experts, relay_cap, tile_size),
        [
            shaped((tok_rows, slots), bf16),
            shaped((tok_rows, slots), bf16),
            shaped((tok_rows, dec_width), jnp.float32),
            shaped((relay_slots, tok_rows), bf16),
            shaped((groups, relay_cap), jnp.int32),
        ],
        [ids_later.T, gate_weights.T, target.reshape(1, tok_rows), tokens_later, dec_embed],
        "prep",
        2 * tok_rows * dec_width * model_width,
        room=WIDE_ROOM,
    )
    spots = lax.all_to_all(spots, "expert", split_axis=0, concat_axis=0, tiled=True)
    folded = fold(down_later, dec_embed)
    arrived, high, low, base, relay, folded, spots = lax.optimization_barrier(
        (arrived, high, low, base, relay, folded, spots)
    )
    returned = swap_all(experts_apply(arrived, expert_gate, expert_up, folded, "experts"))
    packed = whole_call(
        functools.partial(combine_kernel, groups, relay_cap),
        [shaped((relay_cap, dec_width), bf16)] * groups,
        [high, low, base, relay] + returned,
        "combine",
        2 * tok_rows * dec_width * (2 * slots + relay_slots),
    )
    landed = swap_all(packed)
    owner = lax.axis_index("expert")
    band_row = lax.axis_index("dp")
    row_ids = band_row * tile_height + jnp.arange(tile_height, dtype=jnp.int32)
    col_ids = owner * tile_width + jnp.arange(tile_width, dtype=jnp.int32)
    row_table, col_table = positional(row_ids, col_ids, dec_width)
    edge = 16
    grid_shape = (tile_height, tile_width, dec_width)
    normed, decoder_in, keep, top, bottom, first, last = whole_call(
        functools.partial(place_kernel, groups),
        [
            shaped(grid_shape, bf16),
            shaped(grid_shape, jnp.float32),
            shaped((tile_height, tile_width, 1), jnp.float32),
            shaped((RAD, tile_width, dec_width), bf16),
            shaped((RAD, tile_width, dec_width), bf16),
            shaped((tile_height, edge, dec_width), bf16),
            shaped((tile_height, edge, dec_width), bf16),
        ],
        [spots, mask_token.reshape(1, dec_width), row_table, col_table, norm_gain.reshape(1, dec_width)] + landed,
        "place",
        2 * tile_size * relay_slots * dec_width,
    )
    bands = lax.axis_size("dp")
    upward = [(i + 1, i) for i in range(bands - 1)]
    downward = [(i, i + 1) for i in range(bands - 1)]
    before = lax.ppermute(last, "expert", [(i, i + 1) for i in range(groups - 1)])
    after = lax.ppermute(first, "expert", [(i + 1, i) for i in range(groups - 1)])
    sides = jnp.concatenate([before[:, edge // 2 :], after[:, : edge // 2]], 1)
    bottom = jnp.concatenate([bottom, sides[tile_height - RAD :]], 1)
    top = jnp.concatenate([top, sides[:RAD]], 1)
    above = lax.ppermute(bottom, "dp", downward)
    below = lax.ppermute(top, "dp", upward)
    grid_height = tile_height * bands
    grid_width = tile_width * groups
    cols = -(-(tile_width - STRIP + SPAN) // 16) * 16
    inner_shape = (tile_height - 2 * RAD, tile_width, dec_width)
    queries, kv, decoded_inner, d_attn_inner, loss_inner = whole_call(
        functools.partial(inner_kernel, grid_height, grid_width),
        [
            shaped(grid_shape, bf16),
            shaped((tile_height, cols, 2 * dec_width), bf16),
            shaped(inner_shape, bf16),
            shaped(inner_shape, bf16),
            shaped((1, 1), jnp.float32),
        ],
        [normed, before, after, decoder_in, keep, w_qkv, w_out, w_head, pixels],
        "inner",
        10 * tile_size * dec_width * dec_width,
        [
            pltpu.VMEM(grid_shape, bf16),
            pltpu.VMEM((tile_height - 2 * RAD, tile_width, PD), bf16),
            pltpu.SemaphoreType.DMA(()),
        ],
        room=INNER_ROOM,
        last=pl.BlockSpec(memory_space=pl.ANY),
    )
    return whole_call(
        functools.partial(outer_kernel, grid_height, grid_width),
        [shaped(grid_shape, bf16), shaped(grid_shape, bf16), shaped((1, 1), jnp.float32)],
        [above, below, queries, kv, decoded_inner, d_attn_inner, loss_inner]
        + [decoder_in, keep, pixels, w_qkv, w_out, w_head],
        "outer",
        12 * tile_size * dec_width * dec_width,
        [
            pltpu.VMEM((tile_height + 2 * RAD, cols, 2 * dec_width), bf16),
            pltpu.VMEM(grid_shape, bf16),
        ],
        room=OUTER_ROOM,
    )

def solution(mesh):
    in_specs = (
        P(("dp", "expert"), None),
        P(("dp", "expert"), None),
        P(("dp", "expert"), None),
        P(("dp", "expert")),
        P("expert", None, None),
        P("expert", None, None),
        P("expert", None, None),
        P(),
        P(),
        P(),
        P(),
        P(),
        P(),
        P("dp", "expert", None),
    )
    out_specs = (P("dp", "expert", None), P("dp", "expert", None), P("dp", "expert"))
    return jax.shard_map(local, mesh=mesh, in_specs=in_specs, out_specs=out_specs, check_vma=False)
```

```python
import functools
import math

import jax
import jax.numpy as jnp
from jax import lax
from jax.experimental import pallas as pl
from jax.experimental.pallas import tpu as pltpu
from jax.sharding import PartitionSpec as P

TOPK = 2
HD = 32
PD = 768
RAD = 3


EPSILON = 1e-06


def positional(row_ids, col_ids, total_width):
    quarter = total_width // 4
    frequency = jnp.exp(jnp.arange(quarter, dtype=jnp.float32) * (-math.log(10000.0) / quarter))
    row_angle = row_ids.astype(jnp.float32)[:, None] * frequency[None, :]
    col_angle = col_ids.astype(jnp.float32)[:, None] * frequency[None, :]
    return (
        jnp.concatenate([jnp.sin(row_angle), jnp.cos(row_angle)], 1),
        jnp.concatenate([jnp.sin(col_angle), jnp.cos(col_angle)], 1),
    )


def dot(a, b, dims=((1,), (0,))):
    return lax.dot_general(a, b, (dims, ((), ())), preferred_element_type=jnp.float32)


def iota(shape, axis):
    return lax.broadcasted_iota(jnp.int32, shape, axis)


def ones_where(mask):
    return jnp.where(mask, 1.0, 0.0).astype(jnp.bfloat16)


def route_of(width, local_experts, total, axis, shape):
    slot = iota(shape, axis)
    block = slot // (local_experts * width)
    return (block ^ lax.axis_index("expert")) * local_experts + slot // width % local_experts


def slot_matrix(member, width, route):
    buckets, items = member.shape
    total = route.shape[0]
    earlier = ones_where(iota((items, items), 0) < iota((items, items), 1))
    rank = dot(ones_where(member), earlier)
    code = jnp.where(member, rank, -1.0).astype(jnp.bfloat16)
    expand = ones_where(route == iota((total, buckets), 1))
    place = (iota((total, items), 0) % width).astype(jnp.float32)
    return ones_where(dot(expand, code) == place)


def pack_kernel(width, experts, local_experts, ids_ref, tokens_ref, *out_refs):
    items = tokens_ref.shape[0]
    total = experts * width
    member = iota((experts, items), 0) == ids_ref[0:1, :]
    for k in range(1, ids_ref.shape[0]):
        member = member | (iota((experts, items), 0) == ids_ref[k : k + 1, :])
    route = route_of(width, local_experts, total, 0, (total, experts))
    rows = dot(slot_matrix(member, width, route), tokens_ref[...]).astype(jnp.bfloat16)
    share = local_experts * width
    for k, out_ref in enumerate(out_refs):
        out_ref[...] = rows[k * share : (k + 1) * share].reshape(out_ref.shape)


def prep_kernel(
    width, experts, local_experts, relay_cap, tile_size, ids_ref, gates_ref, target_ref, tokens_ref, embed_ref,
    high_ref, low_ref, base_ref, relay_ref, spot_ref,
):
    items = tokens_ref.shape[0]
    slots = high_ref.shape[1]
    lines = iota((experts, items), 0)
    member = jnp.zeros((experts, items), jnp.float32)
    gates = jnp.zeros((experts, items), jnp.float32)
    for k in range(ids_ref.shape[0]):
        hit = ids_ref[k : k + 1, :] == lines
        member = jnp.where(hit, 1.0, member)
        gates = jnp.where(hit, gates_ref[k : k + 1, :], gates)
    earlier = ones_where(iota((items, items), 0) < iota((items, items), 1))
    rank = dot(member.astype(jnp.bfloat16), earlier)
    code = jnp.where(member > 0.5, rank, -1.0).astype(jnp.bfloat16)
    route = route_of(width, local_experts, slots, 1, (experts, slots))
    expand = ones_where(route == iota((experts, slots), 0))
    place = (iota((items, slots), 1) % width).astype(jnp.float32)
    across = ((0,), (0,))
    taken = dot(code, expand, across) == place
    high = gates.astype(jnp.bfloat16)
    low = (gates - high.astype(jnp.float32)).astype(jnp.bfloat16)
    high_ref[...] = jnp.where(taken, dot(high, expand, across), 0.0).astype(jnp.bfloat16)
    low_ref[...] = jnp.where(taken, dot(low, expand, across), 0.0).astype(jnp.bfloat16)
    base_ref[...] = dot(tokens_ref[...], embed_ref[...])
    target = target_ref[...]
    relay_slots = relay_ref.shape[0]
    groups = relay_slots // relay_cap
    me = lax.axis_index("expert")
    route = iota((relay_slots, groups), 0) // relay_cap ^ me
    relay = slot_matrix(iota((groups, items), 0) == target // tile_size, relay_cap, route)
    relay_ref[...] = relay
    spot = target % tile_size
    line = iota((8, items), 0)
    digits = jnp.where(line == 0, spot // 256, jnp.where(line == 1, spot % 256, 1)).astype(jnp.float32)
    found = dot(digits.astype(jnp.bfloat16), relay, ((1,), (1,)))
    spots = jnp.where(found[2:3] > 0.5, found[0:1] * 256.0 + found[1:2], -1.0).astype(jnp.int32)
    for k in range(groups):
        spot_ref[pl.ds(me ^ k, 1), :] = spots[:, k * relay_cap : (k + 1) * relay_cap]


def fold_kernel(down_ref, embed_ref, folded_ref):
    folded_ref[0] = dot(down_ref[0], embed_ref[...]).astype(jnp.bfloat16)


def fold(down, embed):
    local_experts, hidden, model_width = down.shape
    out_width = embed.shape[1]
    chunk = hidden // 2
    return pl.pallas_call(
        fold_kernel,
        grid=(local_experts, hidden // chunk),
        out_shape=shaped((local_experts, hidden, out_width), jnp.bfloat16),
        in_specs=[
            pl.BlockSpec((1, chunk, model_width), lambda e, f: (e, f, 0)),
            pl.BlockSpec((model_width, out_width), lambda e, f: (0, 0)),
        ],
        out_specs=pl.BlockSpec((1, chunk, out_width), lambda e, f: (e, f, 0)),
        compiler_params=pltpu.CompilerParams(vmem_limit_bytes=WIDE_ROOM),
        cost_estimate=pl.CostEstimate(
            flops=2 * local_experts * hidden * model_width * out_width,
            bytes_accessed=2 * math.prod(down.shape),
            transcendentals=0,
        ),
        name="fold",
    )(down, embed)


def ffn_kernel(sources, *refs):
    row_refs, (gate_ref, up_ref, down_ref) = refs[:sources], refs[sources : sources + 3]
    out_refs = refs[sources + 3 :]
    width = row_refs[0].shape[1]
    rows = jnp.concatenate([ref[0] for ref in row_refs], 0)
    gate = dot(rows, gate_ref[0])
    up = dot(rows, up_ref[0])
    hidden = (gate / (1.0 + jnp.exp(-gate)) * up).astype(jnp.bfloat16)
    done = dot(hidden, down_ref[0]).astype(jnp.bfloat16)
    for k, ref in enumerate(out_refs):
        ref[0] = done[k * width : (k + 1) * width]


def combine_kernel(groups, relay_cap, high_ref, low_ref, base_ref, relay_ref, *refs):
    back = jnp.concatenate([ref[...].reshape(-1, ref.shape[-1]) for ref in refs[:groups]], 0)
    embedded = base_ref[...] + dot(high_ref[...], back) + dot(low_ref[...], back)
    packed = dot(relay_ref[...], embedded.astype(jnp.bfloat16)).astype(jnp.bfloat16)
    for k, ref in enumerate(refs[groups:]):
        ref[...] = packed[k * relay_cap : (k + 1) * relay_cap]


def place_kernel(groups, spot_ref, mask_ref, row_ref, col_ref, gain_ref, *refs):
    landed_refs = refs[:groups]
    normed_ref, dec_ref, keep_ref, low_ref, high_ref, first_ref, last_ref = refs[groups:]
    height, breadth, width = normed_ref.shape
    half = width // 2
    me = lax.axis_index("expert")
    spot = jnp.concatenate([spot_ref[pl.ds(me ^ k, 1), :] for k in range(groups)], 1)
    landed = jnp.concatenate([ref[...] for ref in landed_refs], 0)
    slots = landed.shape[0]
    rim = low_ref.shape[0]
    edge = first_ref.shape[1]
    for r in range(height):
        hit = spot == iota((breadth, slots), 0) + r * breadth
        ones = jnp.where(hit, 1.0, 0.0)
        keep = jnp.sum(ones, axis=1, keepdims=True)
        seen = dot(ones.astype(jnp.bfloat16), landed)
        seen = jnp.where(keep > 0.5, seen, mask_ref[...].astype(jnp.float32))
        left = seen[:, :half] + row_ref[r : r + 1, :]
        right = seen[:, half:] + col_ref[...]
        state = jnp.concatenate([left, right], 1)
        square = jnp.sum(state * state, axis=1, keepdims=True) * (1.0 / width)
        normed = (state * lax.rsqrt(square + EPSILON) * gain_ref[...]).astype(jnp.bfloat16)
        normed_ref[r] = normed
        dec_ref[r] = state
        keep_ref[r] = keep
        first_ref[r] = normed[:edge]
        last_ref[r] = normed[breadth - edge :]
        if r < rim:
            low_ref[r] = normed
        if r >= height - rim:
            high_ref[r - height + rim] = normed


VM = pl.BlockSpec(memory_space=pltpu.VMEM)
ROOM = 16 * 2**20
WIDE_ROOM = 56 * 2**20


def whole_call(kernel, outs, ins, name, flops, scratch=(), room=ROOM, last=VM):
    size = sum(math.prod(a.shape) * a.dtype.itemsize for a in tuple(outs) + tuple(ins))
    return pl.pallas_call(
        kernel,
        out_shape=tuple(outs),
        in_specs=[VM] * (len(ins) - 1) + [last],
        out_specs=tuple([VM] * len(outs)),
        scratch_shapes=list(scratch),
        compiler_params=pltpu.CompilerParams(vmem_limit_bytes=room),
        cost_estimate=pl.CostEstimate(flops=flops, bytes_accessed=size, transcendentals=0),
        name=name,
    )(*ins)


def shaped(shape, dtype):
    return jax.ShapeDtypeStruct(shape, dtype)


def experts_apply(blocks, gate, up, down, name):
    sources = len(blocks)
    local_experts, width, model_width = blocks[0].shape
    hidden = gate.shape[2]
    out_width = down.shape[2]
    each = lambda *shape: pl.BlockSpec((1,) + shape, lambda e: (e, 0, 0))
    return pl.pallas_call(
        functools.partial(ffn_kernel, sources),
        grid=(local_experts,),
        out_shape=[shaped((local_experts, width, out_width), jnp.bfloat16)] * sources,
        in_specs=[each(width, model_width)] * sources
        + [each(model_width, hidden), each(model_width, hidden), each(hidden, out_width)],
        out_specs=[each(width, out_width)] * sources,
        compiler_params=pltpu.CompilerParams(vmem_limit_bytes=WIDE_ROOM),
        cost_estimate=pl.CostEstimate(
            flops=2 * sources * local_experts * width * hidden * (2 * model_width + out_width),
            bytes_accessed=2 * local_experts * hidden * (2 * model_width + out_width),
            transcendentals=0,
        ),
        name=name,
    )(*blocks, gate, up, down)


INNER_ROOM = 32 * 2**20
OUTER_ROOM = 32 * 2**20
SPAN = 32
STRIP = 16


def shift_matrix(cols, total, groups):
    p, q = iota((cols, total), 0), iota((cols, total), 1)
    hit = jnp.zeros((cols, total), jnp.bool_)
    for start, count, origin in groups:
        hit = hit | ((p >= start) & (p < start + count) & (q - origin == p - start))
    return ones_where(hit)


def attention(q_ref, kv_ref, key_rows, starts, grid_h, grid_w, tile_h, tile_w, sink):
    width = q_ref.shape[2]
    lanes = 256
    heads = lanes // HD
    lane_head = iota((1, lanes), 1) // HD
    masks = [lane_head == h for h in range(heads)]
    picks = [ones_where(m) for m in masks]
    keys = key_rows * SPAN
    scale = math.log2(math.e) / math.sqrt(HD)
    band_row = lax.axis_index("dp")
    owner = lax.axis_index("expert")
    near = []
    for count, q_row, k_row, tile_row in starts:
        qi, ki = iota((count * STRIP, keys), 0), iota((count * STRIP, keys), 1)
        down = ki // SPAN + tile_row - q_row - qi // STRIP
        across = ki % SPAN - qi % STRIP
        ok = (down >= -RAD) & (down <= RAD) & (across >= 0) & (across <= 2 * RAD)
        grid_row = band_row * tile_h + tile_row + ki // SPAN
        near.append((ok & (grid_row >= 0) & (grid_row < grid_h), ki % SPAN))
    for j in range(tile_w // STRIP):
        c0 = j * STRIP
        for (count, q_row, k_row, tile_row), (ok, key_col) in zip(starts, near):
            items = count * STRIP
            grid_col = owner * tile_w + j * STRIP - RAD + key_col
            bias = jnp.where(ok & (grid_col >= 0) & (grid_col < grid_w), 0.0, -1e30)
            for g in range(width // lanes):
                part = slice(g * lanes, (g + 1) * lanes)
                queries = q_ref[q_row : q_row + count, c0 : c0 + STRIP, part].reshape(items, lanes)
                key = kv_ref[k_row : k_row + key_rows, c0 : c0 + SPAN, part].reshape(keys, lanes)
                value = kv_ref[
                    k_row : k_row + key_rows, c0 : c0 + SPAN, width + g * lanes : width + (g + 1) * lanes
                ].reshape(keys, lanes)
                stacked = jnp.concatenate([queries * pick for pick in picks], 0)
                score = dot(stacked, key, ((1,), (1,))).reshape(heads, items, keys)
                weight = jnp.exp2(score * scale + bias[None]).reshape(heads * items, keys)
                total = jnp.sum(weight, axis=1, keepdims=True).reshape(heads, items, 1)
                mixed = dot(weight.astype(jnp.bfloat16), value).reshape(heads, items, lanes)
                over, under = mixed[0], total[0]
                for h in range(1, heads):
                    over = jnp.where(masks[h], mixed[h], over)
                    under = jnp.where(masks[h], total[h], under)
                shape = (count, STRIP, lanes)
                sink((slice(q_row, q_row + count), slice(c0, c0 + STRIP), part), over.reshape(shape), under.reshape(shape))


def finish(rows, att_ref, dec_in_ref, keep_ref, pixels_ref, wout_ref, whead_ref, decoded_ref, dattn_ref, offset):
    breadth, width = att_ref.shape[1:]
    pd = pixels_ref.shape[2]
    bf16 = jnp.bfloat16
    lines = rows.stop - rows.start
    count = lines * breadth
    held = slice(rows.start - offset, rows.stop - offset)
    att = att_ref[rows].reshape(count, width)
    decoded = (dec_in_ref[rows].reshape(count, width) + dot(att, wout_ref[...])).astype(bf16)
    decoded_ref[held] = decoded.reshape(lines, breadth, width)
    pred = dot(decoded, whead_ref[...])
    pix = pixels_ref[held].reshape(count, pd).astype(jnp.float32)
    centred = pix - jnp.sum(pix, axis=1, keepdims=True) * (1.0 / pd)
    spread = jnp.sum(centred * centred, axis=1, keepdims=True) * (1.0 / pd)
    error = (pred - centred * lax.rsqrt(spread + EPSILON)) * (1.0 - keep_ref[rows].reshape(count, 1))
    back = dot(error.astype(bf16), whead_ref[...], ((1,), (1,))).astype(bf16)
    dattn_ref[held] = dot(back, wout_ref[...], ((1,), (1,))).astype(bf16).reshape(lines, breadth, width)
    return jnp.sum(jnp.sum(error * error, axis=1, keepdims=True), axis=0, keepdims=True)


def inner_kernel(
    grid_h, grid_w, normed_ref, before_ref, after_ref, dec_in_ref, keep_ref, wqkv_ref, wout_ref, whead_ref, pixels_ref,
    q_ref, over_ref, under_ref, decoded_ref, dattn_ref, loss_ref, kv_ref, att_ref, held_ref, sem,
):
    height, breadth, width = normed_ref.shape
    cols = kv_ref.shape[1]
    edge = before_ref.shape[1]
    inner = slice(RAD, height - RAD)
    copy = pltpu.make_async_copy(pixels_ref.at[inner], held_ref, sem)
    copy.start()
    shift = shift_matrix(
        cols, breadth + 2 * edge, ((RAD, breadth, 0), (0, RAD, breadth + edge - RAD), (RAD + breadth, RAD, breadth + edge))
    )
    rows = []
    for r in range(height):
        joined = jnp.concatenate([normed_ref[r], before_ref[r], after_ref[r]], 0)
        rows.append(dot(shift, joined).astype(jnp.bfloat16))
    wide = jnp.concatenate(rows, 0)
    kv_ref[...] = dot(wide, wqkv_ref[:, width:]).astype(jnp.bfloat16).reshape(kv_ref.shape)
    flat = normed_ref[...].reshape(height * breadth, width)
    q_ref[...] = dot(flat, wqkv_ref[:, :width]).astype(jnp.bfloat16).reshape(q_ref.shape)
    def keep_sums(place, over, under):
        over_ref[place] = over
        under_ref[place] = under

    starts = [(2, r, 0, 0) for r in range(0, height, 2)]
    attention(q_ref, kv_ref, height, starts, grid_h, grid_w, height, breadth, keep_sums)
    att_ref[inner] = (over_ref[inner] * (1.0 / under_ref[inner])).astype(jnp.bfloat16)
    copy.wait()
    loss_ref[...] = finish(
        inner, att_ref, dec_in_ref, keep_ref, held_ref, wout_ref, whead_ref, decoded_ref, dattn_ref, RAD
    )


def outer_kernel(
    grid_h, grid_w, up_ref, down_ref, q_ref, over_ref, under_ref, decoded_in_ref, dattn_in_ref, loss_in_ref,
    dec_in_ref, keep_ref, pixels_ref, wqkv_ref, wout_ref, whead_ref, decoded_ref, dattn_ref, loss_ref, kv_ref, att_ref,
):
    height, breadth, pd = pixels_ref.shape
    width = q_ref.shape[2]
    cols = kv_ref.shape[1]
    edge = up_ref.shape[1] - breadth
    middle = edge // 2
    bf16 = jnp.bfloat16
    shift = shift_matrix(
        cols, breadth + edge, ((RAD, breadth, 0), (0, RAD, breadth + middle - RAD), (RAD + breadth, RAD, breadth + middle))
    )
    reach = RAD + 1
    blank = jnp.zeros((1,) + kv_ref.shape[1:], bf16)
    kv_ref[0:1] = blank
    kv_ref[2 * reach - 1 : 2 * reach] = blank
    for rim_ref, start in ((up_ref, 1), (down_ref, reach)):
        wide = [dot(shift, rim_ref[r]).astype(bf16) for r in range(RAD)]
        kv = dot(jnp.concatenate(wide, 0), wqkv_ref[:, width:]).astype(bf16)
        kv_ref[start : start + RAD] = kv.reshape(RAD, cols, 2 * width)
    inner = slice(RAD, height - RAD)
    decoded_ref[inner] = decoded_in_ref[...]
    dattn_ref[inner] = dattn_in_ref[...]

    def join(place, over, under):
        att_ref[place] = ((over_ref[place] + over) * (1.0 / (under_ref[place] + under))).astype(bf16)

    starts = [(RAD, 0, 0, -reach), (RAD, height - RAD, reach, height)]
    attention(q_ref, kv_ref, reach, starts, grid_h, grid_w, height, breadth, join)
    loss = loss_in_ref[...]
    for rows in (slice(0, RAD), slice(height - RAD, height)):
        loss = loss + finish(
            rows, att_ref, dec_in_ref, keep_ref, pixels_ref, wout_ref, whead_ref, decoded_ref, dattn_ref, 0
        )
    loss_ref[...] = loss * (0.5 / (height * breadth * pd))


def local(
    tokens,
    expert_ids,
    gate_weights,
    target,
    expert_gate,
    expert_up,
    expert_down,
    dec_embed,
    mask_token,
    norm_gain,
    w_qkv,
    w_out,
    w_head,
    pixels,
):
    groups = lax.axis_size("expert")
    tok_rows = tokens.shape[0]
    model_width = tokens.shape[1]
    local_experts = expert_gate.shape[0]
    experts_all = local_experts * groups
    capacity = 3 * tok_rows * TOPK // (2 * experts_all)
    tile_height = pixels.shape[0]
    tile_width = pixels.shape[1]
    tile_size = tile_height * tile_width
    relay_cap = tile_size // groups
    dec_width = dec_embed.shape[1]
    bf16 = jnp.bfloat16
    width = -(-capacity // 16) * 16
    slots = experts_all * width
    block = shaped((local_experts, width, model_width), bf16)

    def swap(value, k):
        return value if k == 0 else lax.ppermute(value, "expert", [(i, i ^ k) for i in range(groups)])

    def swap_all(values):
        moved = {k: swap(values[k], k) for k in list(range(cut, groups)) + list(range(cut))[::-1]}
        return [moved[k] for k in range(groups)]

    cut = groups * 3 // 4
    outgoing = whole_call(
        functools.partial(pack_kernel, width, experts_all, local_experts),
        [block] * groups,
        [expert_ids.T, tokens],
        "pack",
        2 * slots * tok_rows * model_width,
        room=WIDE_ROOM,
    )
    outgoing, ids_later, tokens_later, down_later = lax.optimization_barrier(
        (outgoing, expert_ids, tokens, expert_down)
    )
    arrived = swap_all(outgoing)
    relay_slots = groups * relay_cap
    high, low, base, relay, spots = whole_call(
        functools.partial(prep_kernel, width, experts_all, local_experts, relay_cap, tile_size),
        [
            shaped((tok_rows, slots), bf16),
            shaped((tok_rows, slots), bf16),
            shaped((tok_rows, dec_width), jnp.float32),
            shaped((relay_slots, tok_rows), bf16),
            shaped((groups, relay_cap), jnp.int32),
        ],
        [ids_later.T, gate_weights.T, target.reshape(1, tok_rows), tokens_later, dec_embed],
        "prep",
        2 * tok_rows * dec_width * model_width,
        room=WIDE_ROOM,
    )
    spots = lax.all_to_all(spots, "expert", split_axis=0, concat_axis=0, tiled=True)
    folded = fold(down_later, dec_embed)
    arrived, high, low, base, relay, folded, spots = lax.optimization_barrier(
        (arrived, high, low, base, relay, folded, spots)
    )
    returned = swap_all(experts_apply(arrived, expert_gate, expert_up, folded, "experts"))
    packed = whole_call(
        functools.partial(combine_kernel, groups, relay_cap),
        [shaped((relay_cap, dec_width), bf16)] * groups,
        [high, low, base, relay] + returned,
        "combine",
        2 * tok_rows * dec_width * (2 * slots + relay_slots),
    )
    landed = swap_all(packed)
    owner = lax.axis_index("expert")
    band_row = lax.axis_index("dp")
    row_ids = band_row * tile_height + jnp.arange(tile_height, dtype=jnp.int32)
    col_ids = owner * tile_width + jnp.arange(tile_width, dtype=jnp.int32)
    row_table, col_table = positional(row_ids, col_ids, dec_width)
    edge = 16
    grid_shape = (tile_height, tile_width, dec_width)
    normed, decoder_in, keep, top, bottom, first, last = whole_call(
        functools.partial(place_kernel, groups),
        [
            shaped(grid_shape, bf16),
            shaped(grid_shape, jnp.float32),
            shaped((tile_height, tile_width, 1), jnp.float32),
            shaped((RAD, tile_width, dec_width), bf16),
            shaped((RAD, tile_width, dec_width), bf16),
            shaped((tile_height, edge, dec_width), bf16),
            shaped((tile_height, edge, dec_width), bf16),
        ],
        [spots, mask_token.reshape(1, dec_width), row_table, col_table, norm_gain.reshape(1, dec_width)] + landed,
        "place",
        2 * tile_size * relay_slots * dec_width,
    )
    bands = lax.axis_size("dp")
    upward = [(i + 1, i) for i in range(bands - 1)]
    downward = [(i, i + 1) for i in range(bands - 1)]
    before = lax.ppermute(last, "expert", [(i, i + 1) for i in range(groups - 1)])
    after = lax.ppermute(first, "expert", [(i + 1, i) for i in range(groups - 1)])
    sides = jnp.concatenate([before[:, edge // 2 :], after[:, : edge // 2]], 1)
    bottom = jnp.concatenate([bottom, sides[tile_height - RAD :]], 1)
    top = jnp.concatenate([top, sides[:RAD]], 1)
    above = lax.ppermute(bottom, "dp", downward)
    below = lax.ppermute(top, "dp", upward)
    grid_height = tile_height * bands
    grid_width = tile_width * groups
    cols = -(-(tile_width - STRIP + SPAN) // 16) * 16
    inner_shape = (tile_height - 2 * RAD, tile_width, dec_width)
    queries, over, under, decoded_inner, d_attn_inner, loss_inner = whole_call(
        functools.partial(inner_kernel, grid_height, grid_width),
        [
            shaped(grid_shape, bf16),
            shaped(grid_shape, jnp.float32),
            shaped(grid_shape, jnp.float32),
            shaped(inner_shape, bf16),
            shaped(inner_shape, bf16),
            shaped((1, 1), jnp.float32),
        ],
        [normed, before, after, decoder_in, keep, w_qkv, w_out, w_head, pixels],
        "inner",
        10 * tile_size * dec_width * dec_width,
        [
            pltpu.VMEM((tile_height, cols, 2 * dec_width), bf16),
            pltpu.VMEM(grid_shape, bf16),
            pltpu.VMEM((tile_height - 2 * RAD, tile_width, PD), bf16),
            pltpu.SemaphoreType.DMA(()),
        ],
        room=INNER_ROOM,
        last=pl.BlockSpec(memory_space=pl.ANY),
    )
    return whole_call(
        functools.partial(outer_kernel, grid_height, grid_width),
        [shaped(grid_shape, bf16), shaped(grid_shape, bf16), shaped((1, 1), jnp.float32)],
        [above, below, queries, over, under, decoded_inner, d_attn_inner, loss_inner]
        + [decoder_in, keep, pixels, w_qkv, w_out, w_head],
        "outer",
        12 * tile_size * dec_width * dec_width,
        [
            pltpu.VMEM((2 * RAD + 2, cols, 2 * dec_width), bf16),
            pltpu.VMEM(grid_shape, bf16),
        ],
        room=OUTER_ROOM,
    )

def solution(mesh):
    in_specs = (
        P(("dp", "expert"), None),
        P(("dp", "expert"), None),
        P(("dp", "expert"), None),
        P(("dp", "expert")),
        P("expert", None, None),
        P("expert", None, None),
        P("expert", None, None),
        P(),
        P(),
        P(),
        P(),
        P(),
        P(),
        P("dp", "expert", None),
    )
    out_specs = (P("dp", "expert", None), P("dp", "expert", None), P("dp", "expert"))
    return jax.shard_map(local, mesh=mesh, in_specs=in_specs, out_specs=out_specs, check_vma=False)
```

```python
import functools
import math

import jax
import jax.numpy as jnp
from jax import lax
from jax.experimental import pallas as pl
from jax.experimental.pallas import tpu as pltpu
from jax.sharding import PartitionSpec as P

TOPK = 2
HD = 32
PD = 768
RAD = 3


EPSILON = 1e-06


def positional(row_ids, col_ids, total_width):
    quarter = total_width // 4
    frequency = jnp.exp(jnp.arange(quarter, dtype=jnp.float32) * (-math.log(10000.0) / quarter))
    row_angle = row_ids.astype(jnp.float32)[:, None] * frequency[None, :]
    col_angle = col_ids.astype(jnp.float32)[:, None] * frequency[None, :]
    return (
        jnp.concatenate([jnp.sin(row_angle), jnp.cos(row_angle)], 1),
        jnp.concatenate([jnp.sin(col_angle), jnp.cos(col_angle)], 1),
    )


def dot(a, b, dims=((1,), (0,))):
    return lax.dot_general(a, b, (dims, ((), ())), preferred_element_type=jnp.float32)


def iota(shape, axis):
    return lax.broadcasted_iota(jnp.int32, shape, axis)


def ones_where(mask):
    return jnp.where(mask, 1.0, 0.0).astype(jnp.bfloat16)


def route_of(width, local_experts, total, axis, shape):
    slot = iota(shape, axis)
    block = slot // (local_experts * width)
    return (block ^ lax.axis_index("expert")) * local_experts + slot // width % local_experts


def slot_matrix(member, width, route):
    buckets, items = member.shape
    total = route.shape[0]
    earlier = ones_where(iota((items, items), 0) < iota((items, items), 1))
    rank = dot(ones_where(member), earlier)
    code = jnp.where(member, rank, -1.0).astype(jnp.bfloat16)
    expand = ones_where(route == iota((total, buckets), 1))
    place = (iota((total, items), 0) % width).astype(jnp.float32)
    return ones_where(dot(expand, code) == place)


def pack_kernel(width, experts, local_experts, ids_ref, tokens_ref, *out_refs):
    items = tokens_ref.shape[0]
    total = experts * width
    member = iota((experts, items), 0) == ids_ref[0:1, :]
    for k in range(1, ids_ref.shape[0]):
        member = member | (iota((experts, items), 0) == ids_ref[k : k + 1, :])
    route = route_of(width, local_experts, total, 0, (total, experts))
    rows = dot(slot_matrix(member, width, route), tokens_ref[...]).astype(jnp.bfloat16)
    share = local_experts * width
    for k, out_ref in enumerate(out_refs):
        out_ref[...] = rows[k * share : (k + 1) * share].reshape(out_ref.shape)


def prep_kernel(
    width, experts, local_experts, relay_cap, tile_size, ids_ref, gates_ref, target_ref, tokens_ref, embed_ref,
    high_ref, low_ref, base_ref, relay_ref, spot_ref,
):
    items = tokens_ref.shape[0]
    slots = high_ref.shape[1]
    lines = iota((experts, items), 0)
    member = jnp.zeros((experts, items), jnp.float32)
    gates = jnp.zeros((experts, items), jnp.float32)
    for k in range(ids_ref.shape[0]):
        hit = ids_ref[k : k + 1, :] == lines
        member = jnp.where(hit, 1.0, member)
        gates = jnp.where(hit, gates_ref[k : k + 1, :], gates)
    earlier = ones_where(iota((items, items), 0) < iota((items, items), 1))
    rank = dot(member.astype(jnp.bfloat16), earlier)
    code = jnp.where(member > 0.5, rank, -1.0).astype(jnp.bfloat16)
    route = route_of(width, local_experts, slots, 1, (experts, slots))
    expand = ones_where(route == iota((experts, slots), 0))
    place = (iota((items, slots), 1) % width).astype(jnp.float32)
    across = ((0,), (0,))
    taken = dot(code, expand, across) == place
    high = gates.astype(jnp.bfloat16)
    low = (gates - high.astype(jnp.float32)).astype(jnp.bfloat16)
    high_ref[...] = jnp.where(taken, dot(high, expand, across), 0.0).astype(jnp.bfloat16)
    low_ref[...] = jnp.where(taken, dot(low, expand, across), 0.0).astype(jnp.bfloat16)
    base_ref[...] = dot(tokens_ref[...], embed_ref[...])
    target = target_ref[...]
    relay_slots = relay_ref.shape[0]
    groups = relay_slots // relay_cap
    me = lax.axis_index("expert")
    route = iota((relay_slots, groups), 0) // relay_cap ^ me
    relay = slot_matrix(iota((groups, items), 0) == target // tile_size, relay_cap, route)
    relay_ref[...] = relay
    spot = target % tile_size
    line = iota((8, items), 0)
    digits = jnp.where(line == 0, spot // 256, jnp.where(line == 1, spot % 256, 1)).astype(jnp.float32)
    found = dot(digits.astype(jnp.bfloat16), relay, ((1,), (1,)))
    spots = jnp.where(found[2:3] > 0.5, found[0:1] * 256.0 + found[1:2], -1.0).astype(jnp.int32)
    for k in range(groups):
        spot_ref[pl.ds(me ^ k, 1), :] = spots[:, k * relay_cap : (k + 1) * relay_cap]


def fold_kernel(down_ref, embed_ref, folded_ref):
    folded_ref[0] = dot(down_ref[0], embed_ref[...]).astype(jnp.bfloat16)


def fold(down, embed):
    local_experts, hidden, model_width = down.shape
    out_width = embed.shape[1]
    chunk = hidden // 2
    return pl.pallas_call(
        fold_kernel,
        grid=(local_experts, hidden // chunk),
        out_shape=shaped((local_experts, hidden, out_width), jnp.bfloat16),
        in_specs=[
            pl.BlockSpec((1, chunk, model_width), lambda e, f: (e, f, 0)),
            pl.BlockSpec((model_width, out_width), lambda e, f: (0, 0)),
        ],
        out_specs=pl.BlockSpec((1, chunk, out_width), lambda e, f: (e, f, 0)),
        compiler_params=pltpu.CompilerParams(vmem_limit_bytes=WIDE_ROOM),
        cost_estimate=pl.CostEstimate(
            flops=2 * local_experts * hidden * model_width * out_width,
            bytes_accessed=2 * math.prod(down.shape),
            transcendentals=0,
        ),
        name="fold",
    )(down, embed)


def ffn_kernel(sources, *refs):
    row_refs, (gate_ref, up_ref, down_ref) = refs[:sources], refs[sources : sources + 3]
    out_refs = refs[sources + 3 :]
    width = row_refs[0].shape[1]
    rows = jnp.concatenate([ref[0] for ref in row_refs], 0)
    gate = dot(rows, gate_ref[0])
    up = dot(rows, up_ref[0])
    hidden = (gate / (1.0 + jnp.exp(-gate)) * up).astype(jnp.bfloat16)
    done = dot(hidden, down_ref[0]).astype(jnp.bfloat16)
    for k, ref in enumerate(out_refs):
        ref[0] = done[k * width : (k + 1) * width]


def combine_kernel(groups, relay_cap, high_ref, low_ref, base_ref, relay_ref, *refs):
    back = jnp.concatenate([ref[...].reshape(-1, ref.shape[-1]) for ref in refs[:groups]], 0)
    embedded = base_ref[...] + dot(high_ref[...], back) + dot(low_ref[...], back)
    packed = dot(relay_ref[...], embedded.astype(jnp.bfloat16)).astype(jnp.bfloat16)
    for k, ref in enumerate(refs[groups:]):
        ref[...] = packed[k * relay_cap : (k + 1) * relay_cap]


def place_kernel(groups, spot_ref, mask_ref, row_ref, col_ref, gain_ref, *refs):
    landed_refs = refs[:groups]
    normed_ref, dec_ref, keep_ref, low_ref, high_ref, first_ref, last_ref = refs[groups:]
    height, breadth, width = normed_ref.shape
    half = width // 2
    me = lax.axis_index("expert")
    spot = jnp.concatenate([spot_ref[pl.ds(me ^ k, 1), :] for k in range(groups)], 1)
    landed = jnp.concatenate([ref[...] for ref in landed_refs], 0)
    slots = landed.shape[0]
    rim = low_ref.shape[0]
    edge = first_ref.shape[1]
    for r in range(height):
        hit = spot == iota((breadth, slots), 0) + r * breadth
        ones = jnp.where(hit, 1.0, 0.0)
        keep = jnp.sum(ones, axis=1, keepdims=True)
        seen = dot(ones.astype(jnp.bfloat16), landed)
        seen = jnp.where(keep > 0.5, seen, mask_ref[...].astype(jnp.float32))
        left = seen[:, :half] + row_ref[r : r + 1, :]
        right = seen[:, half:] + col_ref[...]
        state = jnp.concatenate([left, right], 1)
        square = jnp.sum(state * state, axis=1, keepdims=True) * (1.0 / width)
        normed = (state * lax.rsqrt(square + EPSILON) * gain_ref[...]).astype(jnp.bfloat16)
        normed_ref[r] = normed
        dec_ref[r] = state
        keep_ref[r] = keep
        first_ref[r] = normed[:edge]
        last_ref[r] = normed[breadth - edge :]
        if r < rim:
            low_ref[r] = normed
        if r >= height - rim:
            high_ref[r - height + rim] = normed


VM = pl.BlockSpec(memory_space=pltpu.VMEM)
ROOM = 16 * 2**20
WIDE_ROOM = 56 * 2**20


def whole_call(kernel, outs, ins, name, flops, scratch=(), room=ROOM, last=VM):
    size = sum(math.prod(a.shape) * a.dtype.itemsize for a in tuple(outs) + tuple(ins))
    return pl.pallas_call(
        kernel,
        out_shape=tuple(outs),
        in_specs=[VM] * (len(ins) - 1) + [last],
        out_specs=tuple([VM] * len(outs)),
        scratch_shapes=list(scratch),
        compiler_params=pltpu.CompilerParams(vmem_limit_bytes=room),
        cost_estimate=pl.CostEstimate(flops=flops, bytes_accessed=size, transcendentals=0),
        name=name,
    )(*ins)


def shaped(shape, dtype):
    return jax.ShapeDtypeStruct(shape, dtype)


def experts_apply(blocks, gate, up, down, name):
    sources = len(blocks)
    local_experts, width, model_width = blocks[0].shape
    hidden = gate.shape[2]
    out_width = down.shape[2]
    each = lambda *shape: pl.BlockSpec((1,) + shape, lambda e: (e, 0, 0))
    return pl.pallas_call(
        functools.partial(ffn_kernel, sources),
        grid=(local_experts,),
        out_shape=[shaped((local_experts, width, out_width), jnp.bfloat16)] * sources,
        in_specs=[each(width, model_width)] * sources
        + [each(model_width, hidden), each(model_width, hidden), each(hidden, out_width)],
        out_specs=[each(width, out_width)] * sources,
        compiler_params=pltpu.CompilerParams(vmem_limit_bytes=WIDE_ROOM),
        cost_estimate=pl.CostEstimate(
            flops=2 * sources * local_experts * width * hidden * (2 * model_width + out_width),
            bytes_accessed=2 * local_experts * hidden * (2 * model_width + out_width),
            transcendentals=0,
        ),
        name=name,
    )(*blocks, gate, up, down)


INNER_ROOM = 32 * 2**20
OUTER_ROOM = 32 * 2**20
SPAN = 32
STRIP = 16


def shift_matrix(cols, total, groups):
    p, q = iota((cols, total), 0), iota((cols, total), 1)
    hit = jnp.zeros((cols, total), jnp.bool_)
    for start, count, origin in groups:
        hit = hit | ((p >= start) & (p < start + count) & (q - origin == p - start))
    return ones_where(hit)


def attention(q_ref, kv_ref, key_rows, starts, grid_h, grid_w, tile_h, tile_w, sink):
    width = q_ref.shape[2]
    lanes = 256
    heads = lanes // HD
    lane_head = iota((1, lanes), 1) // HD
    masks = [lane_head == h for h in range(heads)]
    picks = [ones_where(m) for m in masks]
    keys = key_rows * SPAN
    scale = math.log2(math.e) / math.sqrt(HD)
    band_row = lax.axis_index("dp")
    owner = lax.axis_index("expert")
    near = []
    for count, q_row, k_row, tile_row in starts:
        qi, ki = iota((count * STRIP, keys), 0), iota((count * STRIP, keys), 1)
        down = ki // SPAN + tile_row - q_row - qi // STRIP
        across = ki % SPAN - qi % STRIP
        ok = (down >= -RAD) & (down <= RAD) & (across >= 0) & (across <= 2 * RAD)
        grid_row = band_row * tile_h + tile_row + ki // SPAN
        near.append((ok & (grid_row >= 0) & (grid_row < grid_h), ki % SPAN))
    for j in range(tile_w // STRIP):
        c0 = j * STRIP
        for (count, q_row, k_row, tile_row), (ok, key_col) in zip(starts, near):
            items = count * STRIP
            grid_col = owner * tile_w + j * STRIP - RAD + key_col
            bias = jnp.where(ok & (grid_col >= 0) & (grid_col < grid_w), 0.0, -1e30)
            for g in range(width // lanes):
                part = slice(g * lanes, (g + 1) * lanes)
                queries = q_ref[q_row : q_row + count, c0 : c0 + STRIP, part].reshape(items, lanes)
                key = kv_ref[k_row : k_row + key_rows, c0 : c0 + SPAN, part].reshape(keys, lanes)
                value = kv_ref[
                    k_row : k_row + key_rows, c0 : c0 + SPAN, width + g * lanes : width + (g + 1) * lanes
                ].reshape(keys, lanes)
                stacked = jnp.concatenate([queries * pick for pick in picks], 0)
                score = dot(stacked, key, ((1,), (1,))).reshape(heads, items, keys)
                weight = jnp.exp2(score * scale + bias[None]).reshape(heads * items, keys)
                total = jnp.sum(weight, axis=1, keepdims=True).reshape(heads, items, 1)
                mixed = dot(weight.astype(jnp.bfloat16), value).reshape(heads, items, lanes)
                over, under = mixed[0], total[0]
                for h in range(1, heads):
                    over = jnp.where(masks[h], mixed[h], over)
                    under = jnp.where(masks[h], total[h], under)
                shape = (count, STRIP, lanes)
                sink((slice(q_row, q_row + count), slice(c0, c0 + STRIP), part), over.reshape(shape), under.reshape(shape))


def finish(rows, att_ref, dec_in_ref, keep_ref, pixels_ref, wout_ref, whead_ref, decoded_ref, dattn_ref, offset):
    breadth, width = att_ref.shape[1:]
    pd = pixels_ref.shape[2]
    bf16 = jnp.bfloat16
    lines = rows.stop - rows.start
    count = lines * breadth
    held = slice(rows.start - offset, rows.stop - offset)
    att = att_ref[rows].reshape(count, width)
    decoded = (dec_in_ref[rows].reshape(count, width) + dot(att, wout_ref[...])).astype(bf16)
    decoded_ref[held] = decoded.reshape(lines, breadth, width)
    pred = dot(decoded, whead_ref[...])
    pix = pixels_ref[held].reshape(count, pd).astype(jnp.float32)
    centred = pix - jnp.sum(pix, axis=1, keepdims=True) * (1.0 / pd)
    spread = jnp.sum(centred * centred, axis=1, keepdims=True) * (1.0 / pd)
    error = (pred - centred * lax.rsqrt(spread + EPSILON)) * (1.0 - keep_ref[rows].reshape(count, 1))
    back = dot(error.astype(bf16), whead_ref[...], ((1,), (1,))).astype(bf16)
    dattn_ref[held] = dot(back, wout_ref[...], ((1,), (1,))).astype(bf16).reshape(lines, breadth, width)
    return jnp.sum(jnp.sum(error * error, axis=1, keepdims=True), axis=0, keepdims=True)


def inner_kernel(
    grid_h, grid_w, normed_ref, before_ref, after_ref, dec_in_ref, keep_ref, wqkv_ref, wout_ref, whead_ref, pixels_ref,
    q_ref, over_ref, under_ref, decoded_ref, dattn_ref, loss_ref, kv_ref, att_ref, held_ref, sem,
):
    height, breadth, width = normed_ref.shape
    cols = kv_ref.shape[1]
    edge = before_ref.shape[1]
    inner = slice(RAD, height - RAD)
    copy = pltpu.make_async_copy(pixels_ref.at[inner], held_ref, sem)
    copy.start()
    shift = shift_matrix(
        cols, breadth + 2 * edge, ((RAD, breadth, 0), (0, RAD, breadth + edge - RAD), (RAD + breadth, RAD, breadth + edge))
    )
    rows = []
    for r in range(height):
        joined = jnp.concatenate([normed_ref[r], before_ref[r], after_ref[r]], 0)
        rows.append(dot(shift, joined).astype(jnp.bfloat16))
    wide = jnp.concatenate(rows, 0)
    kv_ref[...] = dot(wide, wqkv_ref[:, width:]).astype(jnp.bfloat16).reshape(kv_ref.shape)
    flat = normed_ref[...].reshape(height * breadth, width)
    q_ref[...] = dot(flat, wqkv_ref[:, :width]).astype(jnp.bfloat16).reshape(q_ref.shape)
    def keep_sums(place, over, under):
        over_ref[place] = over
        under_ref[place] = under

    starts = [(height // 2, r, 0, 0) for r in range(0, height, height // 2)]
    attention(q_ref, kv_ref, height, starts, grid_h, grid_w, height, breadth, keep_sums)
    att_ref[inner] = (over_ref[inner] * (1.0 / under_ref[inner])).astype(jnp.bfloat16)
    copy.wait()
    loss_ref[...] = finish(
        inner, att_ref, dec_in_ref, keep_ref, held_ref, wout_ref, whead_ref, decoded_ref, dattn_ref, RAD
    )


def outer_kernel(
    grid_h, grid_w, up_ref, down_ref, q_ref, over_ref, under_ref, decoded_in_ref, dattn_in_ref, loss_in_ref,
    dec_in_ref, keep_ref, pixels_ref, wqkv_ref, wout_ref, whead_ref, decoded_ref, dattn_ref, loss_ref, kv_ref, att_ref,
):
    height, breadth, pd = pixels_ref.shape
    width = q_ref.shape[2]
    cols = kv_ref.shape[1]
    edge = up_ref.shape[1] - breadth
    middle = edge // 2
    bf16 = jnp.bfloat16
    shift = shift_matrix(
        cols, breadth + edge, ((RAD, breadth, 0), (0, RAD, breadth + middle - RAD), (RAD + breadth, RAD, breadth + middle))
    )
    reach = RAD + 1
    blank = jnp.zeros((1,) + kv_ref.shape[1:], bf16)
    kv_ref[0:1] = blank
    kv_ref[2 * reach - 1 : 2 * reach] = blank
    for rim_ref, start in ((up_ref, 1), (down_ref, reach)):
        wide = [dot(shift, rim_ref[r]).astype(bf16) for r in range(RAD)]
        kv = dot(jnp.concatenate(wide, 0), wqkv_ref[:, width:]).astype(bf16)
        kv_ref[start : start + RAD] = kv.reshape(RAD, cols, 2 * width)
    inner = slice(RAD, height - RAD)
    decoded_ref[inner] = decoded_in_ref[...]
    dattn_ref[inner] = dattn_in_ref[...]

    def join(place, over, under):
        att_ref[place] = ((over_ref[place] + over) * (1.0 / (under_ref[place] + under))).astype(bf16)

    starts = [(RAD, 0, 0, -reach), (RAD, height - RAD, reach, height)]
    attention(q_ref, kv_ref, reach, starts, grid_h, grid_w, height, breadth, join)
    loss = loss_in_ref[...]
    for rows in (slice(0, RAD), slice(height - RAD, height)):
        loss = loss + finish(
            rows, att_ref, dec_in_ref, keep_ref, pixels_ref, wout_ref, whead_ref, decoded_ref, dattn_ref, 0
        )
    loss_ref[...] = loss * (0.5 / (height * breadth * pd))


def local(
    tokens,
    expert_ids,
    gate_weights,
    target,
    expert_gate,
    expert_up,
    expert_down,
    dec_embed,
    mask_token,
    norm_gain,
    w_qkv,
    w_out,
    w_head,
    pixels,
):
    groups = lax.axis_size("expert")
    tok_rows = tokens.shape[0]
    model_width = tokens.shape[1]
    local_experts = expert_gate.shape[0]
    experts_all = local_experts * groups
    capacity = 3 * tok_rows * TOPK // (2 * experts_all)
    tile_height = pixels.shape[0]
    tile_width = pixels.shape[1]
    tile_size = tile_height * tile_width
    relay_cap = tile_size // groups
    dec_width = dec_embed.shape[1]
    bf16 = jnp.bfloat16
    width = -(-capacity // 16) * 16
    slots = experts_all * width
    block = shaped((local_experts, width, model_width), bf16)

    def swap(value, k):
        return value if k == 0 else lax.ppermute(value, "expert", [(i, i ^ k) for i in range(groups)])

    def swap_all(values):
        moved = {k: swap(values[k], k) for k in list(range(cut, groups)) + list(range(cut))[::-1]}
        return [moved[k] for k in range(groups)]

    cut = groups * 3 // 4
    outgoing = whole_call(
        functools.partial(pack_kernel, width, experts_all, local_experts),
        [block] * groups,
        [expert_ids.T, tokens],
        "pack",
        2 * slots * tok_rows * model_width,
        room=WIDE_ROOM,
    )
    outgoing, ids_later, tokens_later, down_later = lax.optimization_barrier(
        (outgoing, expert_ids, tokens, expert_down)
    )
    arrived = swap_all(outgoing)
    relay_slots = groups * relay_cap
    high, low, base, relay, spots = whole_call(
        functools.partial(prep_kernel, width, experts_all, local_experts, relay_cap, tile_size),
        [
            shaped((tok_rows, slots), bf16),
            shaped((tok_rows, slots), bf16),
            shaped((tok_rows, dec_width), jnp.float32),
            shaped((relay_slots, tok_rows), bf16),
            shaped((groups, relay_cap), jnp.int32),
        ],
        [ids_later.T, gate_weights.T, target.reshape(1, tok_rows), tokens_later, dec_embed],
        "prep",
        2 * tok_rows * dec_width * model_width,
        room=WIDE_ROOM,
    )
    spots = lax.all_to_all(spots, "expert", split_axis=0, concat_axis=0, tiled=True)
    folded = fold(down_later, dec_embed)
    arrived, high, low, base, relay, folded, spots = lax.optimization_barrier(
        (arrived, high, low, base, relay, folded, spots)
    )
    returned = swap_all(experts_apply(arrived, expert_gate, expert_up, folded, "experts"))
    packed = whole_call(
        functools.partial(combine_kernel, groups, relay_cap),
        [shaped((relay_cap, dec_width), bf16)] * groups,
        [high, low, base, relay] + returned,
        "combine",
        2 * tok_rows * dec_width * (2 * slots + relay_slots),
    )
    landed = swap_all(packed)
    owner = lax.axis_index("expert")
    band_row = lax.axis_index("dp")
    row_ids = band_row * tile_height + jnp.arange(tile_height, dtype=jnp.int32)
    col_ids = owner * tile_width + jnp.arange(tile_width, dtype=jnp.int32)
    row_table, col_table = positional(row_ids, col_ids, dec_width)
    edge = 16
    grid_shape = (tile_height, tile_width, dec_width)
    normed, decoder_in, keep, top, bottom, first, last = whole_call(
        functools.partial(place_kernel, groups),
        [
            shaped(grid_shape, bf16),
            shaped(grid_shape, jnp.float32),
            shaped((tile_height, tile_width, 1), jnp.float32),
            shaped((RAD, tile_width, dec_width), bf16),
            shaped((RAD, tile_width, dec_width), bf16),
            shaped((tile_height, edge, dec_width), bf16),
            shaped((tile_height, edge, dec_width), bf16),
        ],
        [spots, mask_token.reshape(1, dec_width), row_table, col_table, norm_gain.reshape(1, dec_width)] + landed,
        "place",
        2 * tile_size * relay_slots * dec_width,
    )
    bands = lax.axis_size("dp")
    upward = [(i + 1, i) for i in range(bands - 1)]
    downward = [(i, i + 1) for i in range(bands - 1)]
    before = lax.ppermute(last, "expert", [(i, i + 1) for i in range(groups - 1)])
    after = lax.ppermute(first, "expert", [(i + 1, i) for i in range(groups - 1)])
    sides = jnp.concatenate([before[:, edge // 2 :], after[:, : edge // 2]], 1)
    bottom = jnp.concatenate([bottom, sides[tile_height - RAD :]], 1)
    top = jnp.concatenate([top, sides[:RAD]], 1)
    above = lax.ppermute(bottom, "dp", downward)
    below = lax.ppermute(top, "dp", upward)
    grid_height = tile_height * bands
    grid_width = tile_width * groups
    cols = -(-(tile_width - STRIP + SPAN) // 16) * 16
    inner_shape = (tile_height - 2 * RAD, tile_width, dec_width)
    queries, over, under, decoded_inner, d_attn_inner, loss_inner = whole_call(
        functools.partial(inner_kernel, grid_height, grid_width),
        [
            shaped(grid_shape, bf16),
            shaped(grid_shape, jnp.float32),
            shaped(grid_shape, jnp.float32),
            shaped(inner_shape, bf16),
            shaped(inner_shape, bf16),
            shaped((1, 1), jnp.float32),
        ],
        [normed, before, after, decoder_in, keep, w_qkv, w_out, w_head, pixels],
        "inner",
        10 * tile_size * dec_width * dec_width,
        [
            pltpu.VMEM((tile_height, cols, 2 * dec_width), bf16),
            pltpu.VMEM(grid_shape, bf16),
            pltpu.VMEM((tile_height - 2 * RAD, tile_width, PD), bf16),
            pltpu.SemaphoreType.DMA(()),
        ],
        room=INNER_ROOM,
        last=pl.BlockSpec(memory_space=pl.ANY),
    )
    return whole_call(
        functools.partial(outer_kernel, grid_height, grid_width),
        [shaped(grid_shape, bf16), shaped(grid_shape, bf16), shaped((1, 1), jnp.float32)],
        [above, below, queries, over, under, decoded_inner, d_attn_inner, loss_inner]
        + [decoder_in, keep, pixels, w_qkv, w_out, w_head],
        "outer",
        12 * tile_size * dec_width * dec_width,
        [
            pltpu.VMEM((2 * RAD + 2, cols, 2 * dec_width), bf16),
            pltpu.VMEM(grid_shape, bf16),
        ],
        room=OUTER_ROOM,
    )

def solution(mesh):
    in_specs = (
        P(("dp", "expert"), None),
        P(("dp", "expert"), None),
        P(("dp", "expert"), None),
        P(("dp", "expert")),
        P("expert", None, None),
        P("expert", None, None),
        P("expert", None, None),
        P(),
        P(),
        P(),
        P(),
        P(),
        P(),
        P("dp", "expert", None),
    )
    out_specs = (P("dp", "expert", None), P("dp", "expert", None), P("dp", "expert"))
    return jax.shard_map(local, mesh=mesh, in_specs=in_specs, out_specs=out_specs, check_vma=False)
```
